256 devices in a mesh: ctx: 32 (over z, y), tp: 8 (over x, core).
Axes of the slice: x: 4, y: 4, z: 8, core: 2. Of those that a mesh axis runs over, the one named last changes fastest.
Arguments:
- inputs: bfloat16 [8192, 16384], P('ctx', 'tp'), may hold values from -11 to 11
- gate_input: bfloat16 [8192, 16384], P('ctx', 'tp'), may hold values from -6 to 6
- write_proj: bfloat16 [8192, 1024], P('ctx', 'tp'), may hold values from -6 to 6
- read_proj: bfloat16 [8192, 1024], P('ctx', 'tp'), may hold values from -0.5 to 0.5
- step_raw: float32 [256, 8192], P('tp', 'ctx'), may hold values from -1.2 to 1.2
- step_bias: float32 [256], P('tp'), may hold values from -3.3 to -0.1
- decay_log: float32 [256], P('tp')
- skip_gain: float32 [256], P('tp'), may hold values from 0.5 to 1.5
- norm_gain: float32 [16384], P('tp'), may hold values from 0.5 to 1.5
- start_state: float32 [8, 32, 8192], P('tp', 'ctx'), may hold values from -18 to 18
- out_grad: bfloat16 [8192, 16384], P('ctx', 'tp'), may hold values from -11 to 11
Outputs:
- output: bfloat16 [8192, 16384], P('ctx', 'tp')
- final_state: float32 [8, 32, 8192], P('tp', 'ctx')
- grad_inputs: bfloat16 [8192, 16384], P('ctx', 'tp')
- grad_gate: bfloat16 [8192, 16384], P('ctx', 'tp')
- grad_write: bfloat16 [8192, 1024], P('ctx', 'tp')
- grad_read: bfloat16 [8192, 1024], P('ctx', 'tp')
- grad_step: float32 [256, 8192], P('tp', 'ctx')
- grad_heads: float32 [3, 256], P(None, 'tp')
- grad_norm: float32 [16384], P('tp')
The draws below stay inside these ranges and needn't reach their ends.
All inputs are finite; a program needn't handle non-finite values.
Results may differ from the reference program's by a relative error of at most 0.014.
Values sent between devices are 32-bit elements; how exact they have to be, the bound alone decides.
A program may use at most 128 MiB of HBM per device.

```python
import math
import jax
import jax.numpy as jnp
from jax import lax

G = 8
HG = 32
P_SIZE = 64
N = 128
STRETCH = 256
TOK_DEV = 256
TOKENS = 8192
H = 256
INNER = 16384


def head_slow(key):
    picker = jax.random.fold_in(key, 41)
    return jax.random.randint(picker, (G * HG,), 0, 2) == 1


def draw_inputs(key, part):
    width_all = G * HG * P_SIZE
    column = jnp.arange(width_all)
    head_scale = 0.6 + 1.2 * (column // P_SIZE).astype(jnp.float32) / (G * HG - 1)
    sample = jnp.clip(jax.random.normal(jax.random.fold_in(key, 1), (TOKENS, width_all), jnp.float32), -6.0, 6.0)
    return (sample * head_scale).astype(jnp.bfloat16)


def draw_out_grad(key, part):
    width_all = G * HG * P_SIZE
    row = jnp.arange(TOKENS).astype(jnp.float32)
    row_ramp = (0.6 + 1.2 * row / (TOKENS - 1))[:, None]
    sample = jnp.clip(jax.random.normal(jax.random.fold_in(key, 5), (TOKENS, width_all), jnp.float32), -6.0, 6.0)
    return (sample * row_ramp).astype(jnp.bfloat16)


def draw_step_raw(key, part):
    head_count = G * HG
    blocks = TOKENS // TOK_DEV
    offset = jax.random.uniform(jax.random.fold_in(key, 3), (head_count, blocks), jnp.float32, -0.7, 0.7)
    offset = jnp.repeat(offset, TOK_DEV, axis=1)
    jitter = jax.random.uniform(jax.random.fold_in(key, 4), (head_count, TOKENS), jnp.float32, -0.5, 0.5)
    return offset + jitter


def draw_step_bias(key, part):
    slow_heads = head_slow(key)
    uniform_part = jax.random.uniform(jax.random.fold_in(key, 8), (G * HG,), jnp.float32, 0.0, 0.7)
    return jnp.where(slow_heads, -3.3 + uniform_part, -0.8 + uniform_part)


def draw_decay_log(key, part):
    slow_heads = head_slow(key)
    uniform_part = jax.random.uniform(jax.random.fold_in(key, 9), (G * HG,), jnp.float32, -0.4, 0.4)
    fast_level = jnp.log(0.05)
    slow_level = jnp.log(0.33 / (0.05 * TOKENS))
    return jnp.where(slow_heads, slow_level + uniform_part, fast_level + uniform_part)


def shard_levels(stream_key, shape, cuts, smallest, top_value):
    def one(dim, parts):
        steps = jax.random.uniform(jax.random.fold_in(jax.random.fold_in(stream_key, 6), dim), (parts,), jnp.float32, smallest / len(cuts), top_value / len(cuts))
        return jnp.repeat(jnp.exp(steps), shape[dim] // parts).reshape((-1,) + (1,) * (len(shape) - dim - 1))

    loudness = one(*cuts[0])
    for cut in cuts[1:]:
        loudness = loudness * one(*cut)
    return loudness


def centred(own_key, extent, deviation, bound, cuts=(), kind=jnp.bfloat16):
    drawn = jax.random.normal(own_key, extent, jnp.float32) * deviation
    if len(cuts) > 0:
        drawn = shard_levels(own_key, extent, cuts, -0.22, 0.18) * drawn
    return jnp.clip(drawn, min=-bound, max=bound).astype(kind)


def setup_inputs(seed: int = 0) -> dict:
    keys = jax.random.split(jax.random.key(seed), 12)
    inputs = draw_inputs(jax.random.fold_in(keys[11], 71), 0)
    gate_input = centred(keys[1], (TOKENS, INNER), 1.0, 6.0, ((0, 32), (1, 8)))
    write_proj = centred(keys[2], (TOKENS, G * N), 1.0, 6.0, ((0, 32), (1, 8)))
    read_proj = centred(keys[3], (TOKENS, G * N), N ** -0.5, 0.5, ((0, 32), (1, 8)))
    step_raw = draw_step_raw(jax.random.fold_in(keys[11], 71), 0)
    step_bias = draw_step_bias(jax.random.fold_in(keys[11], 71), 0)
    decay_log = draw_decay_log(jax.random.fold_in(keys[11], 71), 0)
    skip_gain = jnp.clip(0.5 + 1.0 * jax.random.uniform(keys[7], (H,), jnp.float32) ** shard_levels(keys[7], (H,), ((0, 8),), -0.2, 0.2), 0.5, 1.5)
    norm_gain = jnp.clip(1.0 + 0.1 * jax.random.normal(keys[8], (INNER,), jnp.float32), 0.5, 1.5)
    start_state = centred(keys[9], (G, HG, P_SIZE * N), 3.0, 18.0, ((0, 8), (1, 32)), jnp.float32)
    out_grad = draw_out_grad(jax.random.fold_in(keys[11], 71), 0)
    return dict(inputs=inputs, gate_input=gate_input, write_proj=write_proj, read_proj=read_proj, step_raw=step_raw, step_bias=step_bias, decay_log=decay_log, skip_gain=skip_gain, norm_gain=norm_gain, start_state=start_state, out_grad=out_grad)


eps_norm = 1e-05
highest = lax.Precision.HIGHEST

def local_parts(inputs, write_proj, read_proj, step_raw, step_bias, decay_log):
    blocks = inputs.shape[0] // STRETCH
    groups = write_proj.shape[1] // N
    head_count = step_raw.shape[0]
    per_group = head_count // groups
    input_blocks = inputs.reshape(blocks, STRETCH, groups, per_group, P_SIZE).astype(jnp.float32)
    write_blocks = write_proj.reshape(blocks, STRETCH, groups, N).astype(jnp.float32)
    read_blocks = read_proj.reshape(blocks, STRETCH, groups, N).astype(jnp.float32)
    step_size = jax.nn.softplus(step_raw + step_bias[:, None]).reshape(groups, per_group, blocks, STRETCH)
    decay_rate = jnp.exp(decay_log).reshape(groups, per_group, 1, 1)
    cumulative = jnp.cumsum(-decay_rate * step_size, axis=3)
    read_write = jnp.einsum('kign,kjgn->gkij', read_blocks, write_blocks, precision=highest)
    log_gap = cumulative[..., :, None] - cumulative[..., None, :]
    causal = jnp.arange(STRETCH)[:, None] >= jnp.arange(STRETCH)[None, :]
    decay_matrix = jnp.exp(jnp.where(causal, log_gap, -1e+30))
    mixing = lax.optimization_barrier((read_write[:, None] * decay_matrix * step_size[..., None, :]).astype(jnp.bfloat16))
    y_intra = jnp.einsum('ghkij,kjghp->kighp', mixing.astype(jnp.float32), input_blocks, precision=highest)
    to_end = jnp.exp(cumulative[..., -1:] - cumulative) * step_size
    write_scaled = lax.optimization_barrier((to_end[..., None] * jnp.moveaxis(write_blocks, 2, 0)[:, None]).astype(jnp.bfloat16))
    stretch_states = jnp.einsum('ghkjn,kjghp->ghkpn', write_scaled.astype(jnp.float32), input_blocks, precision=highest)
    return (y_intra, stretch_states, cumulative)

def read_states(read_proj, cumulative, incoming):
    blocks = read_proj.shape[0] // STRETCH
    groups = incoming.shape[0]
    read_blocks = read_proj.reshape(blocks, STRETCH, groups, N).astype(jnp.float32)
    rounded = lax.optimization_barrier(incoming.astype(jnp.bfloat16)).astype(jnp.float32)
    product = jnp.einsum('kign,ghkpn->kighp', read_blocks, rounded, precision=highest)
    return product * jnp.exp(jnp.transpose(cumulative, (2, 3, 0, 1)))[..., None]

def forward_model(inputs, gate_input, write_proj, read_proj, step_raw, step_bias, decay_log, skip_gain, norm_gain, start_state):
    blocks = TOKENS // STRETCH
    head_count = G * HG

    def one_block(element):
        return local_parts(element[0], element[1], element[2], element[3], step_bias, decay_log)
    pieces = (inputs.reshape(blocks, STRETCH, head_count * P_SIZE), write_proj.reshape(blocks, STRETCH, G * N), read_proj.reshape(blocks, STRETCH, G * N), jnp.moveaxis(step_raw.reshape(head_count, blocks, STRETCH), 1, 0))
    y_intra, stretch_states, cumulative = lax.map(jax.checkpoint(one_block), pieces)
    end_factor = jnp.exp(cumulative[:, :, :, 0, -1])

    def advance(running, element):
        return (end_factor_step(running, element), running)

    def end_factor_step(running, element):
        return element[1][..., None, None] * running + element[0]
    final_state, incoming = lax.scan(advance, start_state.reshape(G, HG, P_SIZE, N), (stretch_states[:, :, :, 0], end_factor))

    def one_read(element):
        return read_states(element[0], element[1], element[2][:, :, None])
    y_inter = lax.map(jax.checkpoint(one_read), (read_proj.reshape(blocks, STRETCH, G * N), cumulative, incoming))
    ssd_out = y_intra.reshape(TOKENS, head_count * P_SIZE) + y_inter.reshape(TOKENS, head_count * P_SIZE) + jnp.repeat(skip_gain, P_SIZE) * inputs.astype(jnp.float32)
    gated_values = ssd_out * jax.nn.silu(gate_input.astype(jnp.float32))
    inverse = lax.rsqrt(lax.optimization_barrier(jnp.mean(gated_values * gated_values, axis=1)) + eps_norm)
    output = (gated_values * inverse[:, None] * norm_gain).astype(jnp.bfloat16)
    return (output, final_state.reshape(G, HG, P_SIZE * N))

def reference(inputs, gate_input, write_proj, read_proj, step_raw, step_bias, decay_log, skip_gain, norm_gain, start_state, out_grad):

    def forward(inputs, gate_input, write_proj, read_proj, step_raw, step_bias, decay_log, skip_gain, norm_gain):
        return forward_model(inputs, gate_input, write_proj, read_proj, step_raw, step_bias, decay_log, skip_gain, norm_gain, start_state)
    output, pullback, final_state = jax.vjp(forward, inputs, gate_input, write_proj, read_proj, step_raw, step_bias, decay_log, skip_gain, norm_gain, has_aux=True)
    gradients = pullback(out_grad)
    grad_scale = 1.0 / math.sqrt(TOKENS)
    grad_heads = jnp.stack([gradients[5], gradients[6], gradients[7]]) * grad_scale
    return (output, final_state, gradients[0], gradients[1], gradients[2], gradients[3], gradients[4], grad_heads, gradients[8] * grad_scale)
```

```python
import functools
import math

import jax
import jax.numpy as jnp
from jax import lax
from jax.experimental import pallas as pl
from jax.experimental.pallas import tpu as pltpu
from jax.sharding import PartitionSpec as P

P_SIZE = 64
N = 128
NY = 4
EPS = 1e-05
F32 = jnp.float32
BF = jnp.bfloat16
MESH = pl.DeviceIdType.MESH


def contract(a, b, da, db):
    return lax.dot_general(a, b, (((da,), (db,)), ((), ())), preferred_element_type=F32)


def nn(a, b):
    return contract(a, b, 1, 0)


def nt(a, b):
    return contract(a, b, 1, 1)


def tn(a, b):
    return contract(a, b, 0, 0)


def split3(a):
    hi = a.astype(BF)
    rest = a - hi.astype(F32)
    mid = rest.astype(BF)
    return hi, mid, (rest - mid.astype(F32)).astype(BF)


def nn3(a, b):
    hi, mid, lo = split3(a)
    return nn(hi, b) + (nn(mid, b) + nn(lo, b))


def iota(shape, dim):
    return lax.broadcasted_iota(jnp.int32, shape, dim)


def kernel(
    ny,
    nz,
    ntp,
    x_ref,
    g_ref,
    w_ref,
    r_ref,
    raw_ref,
    bias_ref,
    decay_ref,
    skip_ref,
    gain_ref,
    start_ref,
    og_ref,
    out_ref,
    fin_ref,
    dx_ref,
    dg_ref,
    dw_ref,
    dr_ref,
    dstep_ref,
    dheads_ref,
    dnorm_ref,
    st_hi,
    st_mid,
    lhs_ref,
    rhs_ref,
    ahl_ref,
    dl_row,
    te_ref,
    e_ref,
    dl_ref,
    xs_ref,
    ssd_ref,
    sig_ref,
    v_ref,
    d_ref,
    de_ref,
    dxi_ref,
    rwm_ref,
    rwt_ref,
    drwt_ref,
    acc_ref,
    invk_ref,
    rk_ref,
    dwr_ref,
    sk_ref,
    es_ref,
    s_buf,
    s_in,
    t_buf,
    t_in,
    zb_buf,
    zb_in,
    yb_buf,
    yb_in,
    g_buf,
    g_in,
    u_buf,
    u_in,
    vb_buf,
    vb_in,
    wb_buf,
    wb_in,
    tp_buf,
    tp_in,
    ny_buf,
    ny_in,
    nz_buf,
    nz_in,
    ly_buf,
    ly_in,
    lz_buf,
    lz_in,
    ssem,
    rsem,
):
    toks, cols_all = x_ref.shape
    heads = raw_ref.shape[0]
    pairs = heads // 2
    half = toks // 2
    inner = cols_all * ntp
    ctx = lax.axis_index("ctx")
    tp = lax.axis_index("tp")
    y = lax.rem(ctx, ny)
    z = lax.div(ctx, ny)

    def along_y(to):
        return {"ctx": z * ny + to}

    def along_z(to):
        return {"ctx": to * ny + y}

    def along_t(to):
        return {"tp": to}

    lines = {"y": (ny, y, along_y), "z": (nz, z, along_z), "t": (ntp, tp, along_t)}

    barrier = pltpu.get_barrier_semaphore()
    partners = 0
    for count, me, where in lines.values():
        for d in range(1, count):
            pl.semaphore_signal(
                barrier,
                inc=1,
                device_id=where(lax.rem(me + d, count)),
                device_id_type=MESH,
            )
            partners += 1
    pl.semaphore_wait(barrier, partners)

    def exchange(slot, line, src, dst, spread):
        count, me, where = lines[line]
        made = []
        for d in range(1, count):
            to = lax.rem(me + d, count)
            made.append(
                pltpu.make_async_remote_copy(
                    src_ref=src.at[to] if spread else src,
                    dst_ref=dst.at[d],
                    send_sem=ssem.at[slot, d],
                    recv_sem=rsem.at[slot, d],
                    device_id=where(to),
                    device_id_type=MESH,
                )
            )
        for c in made:
            c.start()
        return made

    def arrived(made):
        for c in made:
            c.wait_recv()

    def sent(made):
        for c in made:
            c.wait_send()

    def from_y(k):
        return lax.rem(y + ny - k, ny)

    def from_z(k):
        return lax.rem(z + nz - k, nz)

    def cols_of(j):
        return pl.ds(pl.multiple_of(j * N, N), N)

    lane_low = iota((1, N), 1) < P_SIZE

    def lane_head(j):
        return 2 * j + jnp.where(lane_low, 0, 1)

    eye = iota((heads, heads), 0) == iota((heads, heads), 1)

    def column(row):
        return jnp.sum(
            jnp.where(eye, jnp.broadcast_to(row, (heads, heads)), 0.0), axis=1, keepdims=True
        )

    def row_of(col):
        return jnp.sum(
            jnp.where(eye, jnp.broadcast_to(col, (heads, heads)), 0.0), axis=0, keepdims=True
        )

    bias_raw = raw_ref[...] + column(bias_ref[...])
    delta = jnp.maximum(bias_raw, 0.0) + jnp.log1p(jnp.exp(-jnp.abs(bias_raw)))
    rate = jnp.exp(column(decay_ref[...]))
    skip_col = column(skip_ref[...])
    upto = (iota((toks, toks), 0) <= iota((toks, toks), 1)).astype(F32).astype(BF)
    a = nn3(-rate * delta, upto)
    a_end = a[:, toks - 1 : toks]
    dl_row[...] = delta
    stack = [a, jnp.exp(a), jnp.exp(a_end - a) * delta, delta]
    if 4 * heads < N:
        stack.append(jnp.zeros((N - 4 * heads, toks), F32))
    hi, mid, _ = split3(jnp.transpose(jnp.concatenate(stack, axis=0)))
    st_hi[...] = hi
    st_mid[...] = mid
    parts = [p.astype(F32) for p in split3(a)]
    for i in range(3):
        ahl_ref[i] = parts[i]
    tall = parts + [jnp.ones((8, toks), F32), jnp.zeros((N - 3 * heads - 8, toks), F32)]
    lhs_ref[...] = jnp.transpose(jnp.concatenate(tall, axis=0)).astype(BF)

    end_rows = jnp.broadcast_to(a_end, (heads, N))
    for h in range(heads):
        s_buf[h % ny, nz * P_SIZE + h // ny : nz * P_SIZE + h // ny + 1, :] = end_rows[h : h + 1, :]
    if nz < 8:
        for k in range(ny):
            s_buf[k, nz * P_SIZE + nz :, :] = jnp.zeros((8 - nz, N), F32)

    def put_heads(buf, j, both):
        for i in range(2):
            h = 2 * j + i
            rows = pl.ds(pl.multiple_of(lax.div(h, ny) * P_SIZE, P_SIZE), P_SIZE)
            buf[lax.rem(h, ny), rows, :] = both[i * P_SIZE : (i + 1) * P_SIZE, :]

    def take_heads(buf, j):
        got = []
        for i in range(2):
            h = 2 * j + i
            rows = pl.ds(pl.multiple_of(lax.div(h, ny) * P_SIZE, P_SIZE), P_SIZE)
            got.append(buf[from_y(lax.rem(h, ny)), rows, :])
        return jnp.concatenate(got, axis=0)

    def take_own(buf, j):
        got = []
        for i in range(2):
            h = 2 * j + i
            rows = pl.ds(pl.multiple_of(lax.div(h, ny) * P_SIZE, P_SIZE), P_SIZE)
            got.append(buf[lax.rem(h, ny), rows, :])
        return jnp.concatenate(got, axis=0)

    def first(j, _):
        cols = cols_of(j)
        place = jnp.concatenate(
            [(iota((N, N), 0) == q * heads + lane_head(j)).astype(F32) for q in (1, 2, 3)], axis=1
        ).astype(BF)
        wide = nn(st_hi[...], place) + nn(st_mid[...], place)
        e_ref[:, cols] = wide[:, :N]
        te_ref[:, cols] = wide[:, N : 2 * N]
        dl_ref[:, cols] = wide[:, 2 * N :]
        scaled = (x_ref[:, cols].astype(F32) * wide[:, N : 2 * N]).astype(BF)
        xs_ref[:, cols] = scaled
        put_heads(s_buf, j, tn(scaled, w_ref[...]))
        return 0

    lax.fori_loop(0, pairs, first, 0)
    y_there = exchange(0, "y", s_buf, s_in, True)
    s_in[0] = s_buf[y]

    causal = iota((toks, toks), 0) >= iota((toks, toks), 1)
    rwm_ref[...] = jnp.where(causal, nt(r_ref[...], w_ref[...]), 0.0)
    rwt_ref[...] = jnp.where(
        iota((toks, toks), 0) <= iota((toks, toks), 1), nt(w_ref[...], r_ref[...]), 0.0
    )

    def intra(j, _):
        cols = cols_of(j)
        xp = x_ref[:, cols]
        made = []
        row = iota((N, toks), 0)
        for i in range(2):
            h = 2 * j + i
            rhs = jnp.where((row == h) | (row == heads + h) | (row == 2 * heads + h), 1.0, 0.0)
            for k in range(3):
                rhs = jnp.where(row == 3 * heads + k, -ahl_ref[k, pl.ds(h, 1), :], rhs)
            rhs = rhs.astype(BF)
            rhs_ref[h] = rhs
            d_row = dl_row[pl.ds(h, 1), :]
            gap = nn(lhs_ref[:half, :], rhs[:, :half])
            m = (rwm_ref[:half, :half] * jnp.exp(jnp.minimum(gap, 0.0)) * d_row[:, :half]).astype(BF)
            top = nn(m, xp[:half])
            gap = nn(lhs_ref[half:, :], rhs)
            m = (rwm_ref[half:, :] * jnp.exp(jnp.minimum(gap, 0.0)) * d_row).astype(BF)
            made.append(jnp.concatenate([top, nn(m, xp)], axis=0))
        yi = jnp.where(lane_low, made[0], made[1])
        skip_row = jnp.sum(
            jnp.where(iota((heads, N), 0) == lane_head(j), skip_col, 0.0), axis=0, keepdims=True
        )
        ssd_ref[:, cols] = yi + skip_row * xp.astype(F32)
        gate = g_ref[:, cols].astype(F32)
        sig_ref[:, cols] = 1.0 / (1.0 + jnp.exp(-gate))
        return 0

    lax.fori_loop(0, pairs, intra, 0)
    arrived(y_there)

    def rows_z(k):
        return slice(k * P_SIZE, (k + 1) * P_SIZE)

    def log_end(k, j):
        return s_in[from_y(k), nz * P_SIZE + j : nz * P_SIZE + j + 1, :]

    for j in range(nz):
        total = s_in[from_y(0), rows_z(j), :]
        log_sum = log_end(0, j)
        for k in range(1, ny):
            total = jnp.exp(log_end(k, j)) * total + s_in[from_y(k), rows_z(j), :]
            log_sum = log_sum + log_end(k, j)
        t_buf[j, :P_SIZE, :] = total
        t_buf[j, P_SIZE:, :] = jnp.broadcast_to(log_sum, (8, N))
    z_there = exchange(1, "z", t_buf, t_in, True)
    t_in[0] = t_buf[z]
    arrived(z_there)

    state = start_ref[...]
    for k in range(nz):
        zb_buf[k] = state
        here = from_z(k)
        state = jnp.exp(t_in[here, P_SIZE : P_SIZE + 1, :]) * state + t_in[here, :P_SIZE, :]
    fin_ref[...] = state
    z_back = exchange(2, "z", zb_buf, zb_in, True)
    zb_in[0] = zb_buf[z]
    arrived(z_back)

    for j in range(nz):
        state = zb_in[from_z(j)]
        for k in range(ny):
            yb_buf[k, rows_z(j), :] = state
            if k < ny - 1:
                state = jnp.exp(log_end(k, j)) * state + s_in[from_y(k), rows_z(j), :]
    y_back = exchange(3, "y", yb_buf, yb_in, True)
    yb_in[0] = yb_buf[y]
    arrived(y_back)

    acc_ref[...] = jnp.zeros_like(acc_ref)

    def read(j, _):
        cols = cols_of(j)
        inc = take_heads(yb_in, j).astype(BF)
        ssd = ssd_ref[:, cols] + e_ref[:, cols] * nt(r_ref[...], inc)
        ssd_ref[:, cols] = ssd
        v = ssd * (g_ref[:, cols].astype(F32) * sig_ref[:, cols])
        v_ref[:, cols] = v
        acc_ref[0] += v * v
        acc_ref[1] += v * (og_ref[:, cols].astype(F32) * gain_ref[:, cols])
        return 0

    lax.fori_loop(0, pairs, read, 0)
    tp_buf[0:1, :] = jnp.sum(jnp.transpose(acc_ref[0]), axis=0, keepdims=True)
    tp_buf[1:2, :] = jnp.sum(jnp.transpose(acc_ref[1]), axis=0, keepdims=True)
    tp_buf[2:, :] = jnp.zeros((6, toks), F32)
    tp_sums = exchange(4, "t", tp_buf, tp_in, False)
    tp_in[0] = tp_buf[...]
    arrived(tp_sums)
    both = tp_in[0]
    for k in range(1, ntp):
        both = both + tp_in[k]
    inverse = lax.rsqrt(both[0:1, :] / inner + EPS)
    slope = inverse * inverse * inverse * both[1:2, :] / inner
    invk_ref[0] = jnp.transpose(jnp.broadcast_to(inverse, (N, toks)))
    invk_ref[1] = jnp.transpose(jnp.broadcast_to(slope, (N, toks)))

    def back(j, _):
        cols = cols_of(j)
        sg = og_ref[:, cols].astype(F32) * gain_ref[:, cols]
        dv = invk_ref[0] * sg - v_ref[:, cols] * invk_ref[1]
        d = dv * (g_ref[:, cols].astype(F32) * sig_ref[:, cols])
        d_ref[:, cols] = d.astype(BF)
        de = (d * e_ref[:, cols]).astype(BF)
        de_ref[:, cols] = de
        put_heads(g_buf, j, tn(de, r_ref[...]))
        return 0

    lax.fori_loop(0, pairs, back, 0)
    g_there = exchange(5, "y", g_buf, g_in, True)
    g_in[0] = g_buf[y]

    rk_ref[...] = jnp.zeros_like(rk_ref)
    dwr_ref[...] = jnp.zeros_like(dwr_ref)
    drwt_ref[...] = jnp.zeros_like(drwt_ref)

    def skip_of(j):
        return jnp.sum(
            jnp.where(iota((heads, N), 0) == lane_head(j), skip_col, 0.0), axis=0, keepdims=True
        )

    def gather_heads(j, prod):
        place = (
            iota((N, N), 1) == 2 * j + jnp.where(iota((N, N), 0) < P_SIZE, 0, 1)
        ).astype(F32).astype(BF)
        hi = prod.astype(BF)
        lo = (prod - hi.astype(F32)).astype(BF)
        return nn(hi, place) + nn(lo, place)

    def outs(j, _):
        cols = cols_of(j)
        og = og_ref[:, cols].astype(F32)
        gain = gain_ref[:, cols]
        v = v_ref[:, cols]
        ssd = ssd_ref[:, cols]
        vi = v * invk_ref[0]
        out_ref[:, cols] = (vi * gain).astype(BF)
        ny_buf[pl.ds(j, 1), :] = jnp.sum(og * vi, axis=0, keepdims=True)
        dv = invk_ref[0] * (og * gain) - v * invk_ref[1]
        gate = g_ref[:, cols].astype(F32)
        sig = sig_ref[:, cols]
        dg_ref[:, cols] = (dv * ssd * sig * (1.0 + gate * (1.0 - sig))).astype(BF)
        x = x_ref[:, cols].astype(F32)
        d = d_ref[:, cols].astype(F32)
        sk = jnp.sum(dv * (gate * sig) * x, axis=0, keepdims=True)
        sk_ref[pl.ds(2 * j, 1), :] = jnp.where(lane_low, sk, 0.0)
        sk_ref[pl.ds(2 * j + 1, 1), :] = jnp.where(lane_low, 0.0, sk)
        rk_ref[0] += gather_heads(j, d * (ssd - skip_of(j) * x))
        dwr_ref[1] += nn(de_ref[:, cols], take_heads(yb_in, j).astype(BF))
        return 0

    lax.fori_loop(0, pairs, outs, 0)

    def intra_back(j, _):
        cols = cols_of(j)
        dl = dl_ref[:, cols]
        xd = (x_ref[:, cols].astype(F32) * dl).astype(BF)
        dp = d_ref[:, cols]
        made = []
        sums = None
        for i in range(2):
            h = 2 * j + i
            keep = lane_low if i == 0 else jnp.logical_not(lane_low)
            mine = jnp.where(keep, dp.astype(F32), 0.0).astype(BF)
            rhs = rhs_ref[h]
            decay = jnp.exp(jnp.minimum(-nn(lhs_ref[:half, :], rhs), 0.0))
            upper = nt(xd[:half], mine) * decay
            top = nn((rwt_ref[:half, :] * decay).astype(BF), dp)
            decay = jnp.exp(jnp.minimum(-nn(lhs_ref[half:, :], rhs[:, half:]), 0.0))
            lower = nt(xd[half:], mine[half:]) * decay
            low = nn((rwt_ref[half:, half:] * decay).astype(BF), dp[half:])
            made.append(jnp.concatenate([top, low], axis=0))
            sums = (upper, lower) if sums is None else (sums[0] + upper, sums[1] + lower)
        drwt_ref[:half, :] += sums[0]
        drwt_ref[half:, half:] += sums[1]
        dxi_ref[:, cols] = jnp.where(lane_low, made[0], made[1]) * dl
        return 0

    lax.fori_loop(0, pairs, intra_back, 0)
    arrived(g_there)

    for j in range(nz):
        total = g_in[from_y(ny - 1), rows_z(j), :]
        for k in range(ny - 2, -1, -1):
            total = jnp.exp(log_end(k, j)) * total + g_in[from_y(k), rows_z(j), :]
        u_buf[j] = total
    u_there = exchange(6, "z", u_buf, u_in, True)
    u_in[0] = u_buf[z]
    arrived(u_there)
    state = jnp.zeros((P_SIZE, N), F32)
    for k in range(nz - 1, -1, -1):
        vb_buf[k] = state
        here = from_z(k)
        state = jnp.exp(t_in[here, P_SIZE : P_SIZE + 1, :]) * state + u_in[here]
    v_back = exchange(7, "z", vb_buf, vb_in, True)
    vb_in[0] = vb_buf[z]
    arrived(v_back)
    for j in range(nz):
        state = vb_in[from_z(j)]
        for k in range(ny - 1, -1, -1):
            wb_buf[k, rows_z(j), :] = state
            if k > 0:
                state = jnp.exp(log_end(k, j)) * state + g_in[from_y(k), rows_z(j), :]
    w_back = exchange(8, "y", wb_buf, wb_in, True)
    wb_in[0] = wb_buf[y]

    below = iota((toks, toks), 0) <= iota((toks, toks), 1)
    drwt = jnp.where(below, drwt_ref[...], 0.0).astype(BF)
    dr_in = tn(drwt, w_ref[...])
    dr_ref[...] = (dr_in.astype(BF).astype(F32) + dwr_ref[1].astype(BF).astype(F32)).astype(BF)
    dw_in = nn(drwt, r_ref[...])
    skip_sum = row_of(jnp.sum(sk_ref[...], axis=1, keepdims=True))
    ny_buf[pairs:, :] = jnp.zeros((ny_buf.shape[0] - pairs, N), F32)
    ny_buf[pairs : pairs + 1, :heads] = skip_sum
    sums_y = exchange(9, "y", ny_buf, ny_in, False)
    ny_in[0] = ny_buf[...]
    arrived(w_back)
    arrived(sums_y)
    total = ny_in[0]
    for k in range(1, ny):
        total = total + ny_in[k]
    nz_buf[...] = total
    sums_z = exchange(10, "z", nz_buf, nz_in, False)
    nz_in[0] = nz_buf[...]

    def last(j, _):
        cols = cols_of(j)
        later = take_heads(wb_in, j)
        inc = take_heads(yb_in, j)
        own = take_own(s_buf, j)
        for i in range(2):
            h = 2 * j + i
            end = s_buf[lax.rem(h, ny), pl.ds(nz * P_SIZE + lax.div(h, ny), 1), :]
            part = slice(i * P_SIZE, (i + 1) * P_SIZE)
            es_ref[pl.ds(h, 1), :] = jnp.sum(
                later[part] * (jnp.exp(end) * inc[part] + own[part]), axis=0, keepdims=True
            )
        later = later.astype(BF)
        state_part = nt(w_ref[...], later) * te_ref[:, cols]
        intra_part = dxi_ref[:, cols]
        x = x_ref[:, cols].astype(F32)
        rk_ref[1] += gather_heads(j, x * (intra_part + state_part))
        direct = (d_ref[:, cols].astype(F32) * skip_of(j)).astype(BF).astype(F32)
        joined = (intra_part.astype(BF).astype(F32) + state_part.astype(BF).astype(F32)).astype(BF)
        dx_ref[:, cols] = (joined.astype(F32) + direct).astype(BF)
        dwr_ref[0] += nn(xs_ref[:, cols], later)
        return 0

    lax.fori_loop(0, pairs, last, 0)
    dw_ref[...] = (dw_in.astype(BF).astype(F32) + dwr_ref[0].astype(BF).astype(F32)).astype(BF)

    k_rows = jnp.transpose(rk_ref[1])[:heads]
    d_log = jnp.transpose(rk_ref[0])[:heads] - k_rows
    end_sum = jnp.sum(es_ref[...], axis=1, keepdims=True)
    d_log = d_log + jnp.where(iota((heads, toks), 1) == toks - 1, end_sum, 0.0)
    from_on = (iota((toks, toks), 0) >= iota((toks, toks), 1)).astype(F32).astype(BF)
    d_inc = nn3(d_log, from_on)
    d_delta = k_rows / dl_row[...] - rate * d_inc
    again = raw_ref[...] + column(bias_ref[...])
    d_raw = d_delta * (1.0 / (1.0 + jnp.exp(-again)))
    dstep_ref[...] = d_raw
    ly_buf[...] = jnp.zeros_like(ly_buf)
    ly_buf[0:1, :heads] = row_of(jnp.sum(d_raw, axis=1, keepdims=True))
    ly_buf[1:2, :heads] = row_of(jnp.sum(d_inc * (-rate * dl_row[...]), axis=1, keepdims=True))
    late_y = exchange(11, "y", ly_buf, ly_in, False)
    ly_in[0] = ly_buf[...]
    arrived(late_y)
    total = ly_in[0]
    for k in range(1, ny):
        total = total + ly_in[k]
    lz_buf[...] = total
    late_z = exchange(12, "z", lz_buf, lz_in, False)
    lz_in[0] = lz_buf[...]
    arrived(sums_z)
    arrived(late_z)
    scale = 1.0 / math.sqrt(toks * ny * nz)
    total = nz_in[0]
    late = lz_in[0]
    for k in range(1, nz):
        total = total + nz_in[k]
        late = late + lz_in[k]
    for j in range(pairs):
        dnorm_ref[0:1, j * N : (j + 1) * N] = total[j : j + 1, :] * scale
    dheads_ref[0:2, :] = late[0:2, :heads] * scale
    dheads_ref[2:3, :] = total[pairs : pairs + 1, :heads] * scale
    for made in (
        y_there,
        z_there,
        z_back,
        y_back,
        tp_sums,
        g_there,
        u_there,
        v_back,
        w_back,
        sums_y,
        sums_z,
        late_y,
        late_z,
    ):
        sent(made)


def solution(mesh):
    nctx, ntp = mesh.shape["ctx"], mesh.shape["tp"]
    ny, nz = NY, nctx // NY

    def on_device(
        inputs,
        gate_input,
        write_proj,
        read_proj,
        step_raw,
        step_bias,
        decay_log,
        skip_gain,
        norm_gain,
        start_state,
        out_grad,
    ):
        toks, cols = inputs.shape
        heads = step_raw.shape[0]
        pairs = heads // 2
        group = nz * P_SIZE
        f32, bf = F32, BF

        def v(shape, dtype=f32):
            return pltpu.VMEM(shape, dtype)

        scratch = [
            v((toks, N), bf),
            v((toks, N), bf),
            v((toks, N), bf),
            v((heads, N, toks), bf),
            v((3, heads, toks)),
            v((heads, toks)),
            v((toks, cols)),
            v((toks, cols)),
            v((toks, cols)),
            v((toks, cols), bf),
            v((toks, cols)),
            v((toks, cols)),
            v((toks, cols)),
            v((toks, cols), bf),
            v((toks, cols), bf),
            v((toks, cols)),
            v((toks, toks)),
            v((toks, toks)),
            v((toks, toks)),
            v((2, toks, N)),
            v((2, toks, N)),
            v((2, toks, N)),
            v((2, toks, N)),
            v((heads, N)),
            v((heads, N)),
            v((ny, group + 8, N)),
            v((ny, group + 8, N)),
            v((nz, P_SIZE + 8, N)),
            v((nz, P_SIZE + 8, N)),
            v((nz, P_SIZE, N)),
            v((nz, P_SIZE, N)),
            v((ny, group, N)),
            v((ny, group, N)),
            v((ny, group, N)),
            v((ny, group, N)),
            v((nz, P_SIZE, N)),
            v((nz, P_SIZE, N)),
            v((nz, P_SIZE, N)),
            v((nz, P_SIZE, N)),
            v((ny, group, N)),
            v((ny, group, N)),
            v((8, toks)),
            v((ntp, 8, toks)),
            v((pairs + 8, N)),
            v((ny, pairs + 8, N)),
            v((pairs + 8, N)),
            v((nz, pairs + 8, N)),
            v((8, N)),
            v((ny, 8, N)),
            v((8, N)),
            v((nz, 8, N)),
            pltpu.SemaphoreType.DMA((13, 8)),
            pltpu.SemaphoreType.DMA((13, 8)),
        ]
        vmem = pl.BlockSpec(memory_space=pltpu.VMEM)
        shapes = [
            jax.ShapeDtypeStruct((toks, cols), bf),
            jax.ShapeDtypeStruct((P_SIZE, N), f32),
            jax.ShapeDtypeStruct((toks, cols), bf),
            jax.ShapeDtypeStruct((toks, cols), bf),
            jax.ShapeDtypeStruct((toks, N), bf),
            jax.ShapeDtypeStruct((toks, N), bf),
            jax.ShapeDtypeStruct((heads, toks), f32),
            jax.ShapeDtypeStruct((3, heads), f32),
            jax.ShapeDtypeStruct((1, cols), f32),
        ]
        made = pl.pallas_call(
            functools.partial(kernel, ny, nz, ntp),
            out_shape=shapes,
            in_specs=[vmem] * 11,
            out_specs=[vmem] * 9,
            scratch_shapes=scratch,
            compiler_params=pltpu.CompilerParams(
                collective_id=0, has_side_effects=True, vmem_limit_bytes=60 * 2**20
            ),
        )(
            inputs,
            gate_input,
            write_proj,
            read_proj,
            step_raw,
            step_bias.reshape(1, heads),
            decay_log.reshape(1, heads),
            skip_gain.reshape(1, heads),
            norm_gain.reshape(1, cols),
            start_state.reshape(P_SIZE, N),
            out_grad,
        )
        output, final, dx, dg, dw, dr, dstep, dheads, dnorm = made
        return (
            output,
            final.reshape(1, 1, P_SIZE * N),
            dx,
            dg,
            dw,
            dr,
            dstep,
            dheads,
            dnorm.reshape(cols),
        )

    in_specs = (
        P("ctx", "tp"),
        P("ctx", "tp"),
        P("ctx", "tp"),
        P("ctx", "tp"),
        P("tp", "ctx"),
        P("tp"),
        P("tp"),
        P("tp"),
        P("tp"),
        P("tp", "ctx", None),
        P("ctx", "tp"),
    )
    out_specs = (
        P("ctx", "tp"),
        P("tp", "ctx", None),
        P("ctx", "tp"),
        P("ctx", "tp"),
        P("ctx", "tp"),
        P("ctx", "tp"),
        P("tp", "ctx"),
        P(None, "tp"),
        P("tp"),
    )
    return jax.shard_map(
        on_device, mesh=mesh, in_specs=in_specs, out_specs=out_specs, check_vma=False
    )
```

```python
import functools
import math

import jax
import jax.numpy as jnp
from jax import lax
from jax.experimental import pallas as pl
from jax.experimental.pallas import tpu as pltpu
from jax.sharding import PartitionSpec as P

P_SIZE = 64
N = 128
NY = 4
EPS = 1e-05
SLOTS = 11 + 4 * 4
CHUNKS = 4
UNROLL = 4
F32 = jnp.float32
BF = jnp.bfloat16
MESH = pl.DeviceIdType.MESH


def contract(a, b, da, db):
    return lax.dot_general(a, b, (((da,), (db,)), ((), ())), preferred_element_type=F32)


def nn(a, b):
    return contract(a, b, 1, 0)


def nt(a, b):
    return contract(a, b, 1, 1)


def tn(a, b):
    return contract(a, b, 0, 0)


def split3(a):
    hi = a.astype(BF)
    rest = a - hi.astype(F32)
    mid = rest.astype(BF)
    return hi, mid, (rest - mid.astype(F32)).astype(BF)


def nn3(a, b):
    hi, mid, lo = split3(a)
    return nn(hi, b) + (nn(mid, b) + nn(lo, b))


def iota(shape, dim):
    return lax.broadcasted_iota(jnp.int32, shape, dim)


def kernel(
    ny,
    nz,
    ntp,
    x_ref,
    g_ref,
    w_ref,
    r_ref,
    raw_ref,
    bias_ref,
    decay_ref,
    skip_ref,
    gain_ref,
    start_ref,
    og_ref,
    out_ref,
    fin_ref,
    dx_ref,
    dg_ref,
    dw_ref,
    dr_ref,
    dstep_ref,
    dheads_ref,
    dnorm_ref,
    st_hi,
    st_mid,
    lhs_ref,
    rhs_ref,
    ahl_ref,
    dl_row,
    te_ref,
    e_ref,
    dl_ref,
    xs_ref,
    xd_ref,
    ssd_ref,
    sig_ref,
    v_ref,
    d_ref,
    de_ref,
    dxi_ref,
    rwm_ref,
    rwt_ref,
    drwt_ref,
    acc_ref,
    invk_ref,
    rk_ref,
    dwr_ref,
    sk_ref,
    es_ref,
    lg_buf,
    lg_in,
    lr_buf,
    lr_in,
    f_own,
    f_ref,
    fz_ref,
    s_buf,
    s_in,
    t_buf,
    t_in,
    zb_buf,
    zb_in,
    yb_buf,
    yb_in,
    g_buf,
    g_in,
    u_buf,
    u_in,
    vb_buf,
    vb_in,
    wb_buf,
    wb_in,
    tp_buf,
    tp_in,
    ny_buf,
    ny_in,
    nz_buf,
    nz_in,
    ly_buf,
    ly_in,
    lz_buf,
    lz_in,
    ssem,
    rsem,
):
    toks, cols_all = x_ref.shape
    heads = raw_ref.shape[0]
    pairs = heads // 2
    half = toks // 2
    inner = cols_all * ntp
    ctx = lax.axis_index("ctx")
    tp = lax.axis_index("tp")
    y = lax.rem(ctx, ny)
    z = lax.div(ctx, ny)

    def along_y(to):
        return {"ctx": z * ny + to}

    def along_z(to):
        return {"ctx": to * ny + y}

    def along_t(to):
        return {"tp": to}

    lines = {"y": (ny, y, along_y), "z": (nz, z, along_z), "t": (ntp, tp, along_t)}

    barrier = pltpu.get_barrier_semaphore()
    partners = 0
    for count, me, where in lines.values():
        for d in range(1, count):
            pl.semaphore_signal(
                barrier,
                inc=1,
                device_id=where(lax.rem(me + d, count)),
                device_id_type=MESH,
            )
            partners += 1
    pl.semaphore_wait(barrier, partners)

    slots = iter(range(SLOTS))

    def exchange(line, src, dst):
        slot = next(slots)
        count, me, where = lines[line]
        made = []
        for d in range(1, count):
            to = lax.rem(me + d, count)
            made.append(
                pltpu.make_async_remote_copy(
                    src_ref=src(to),
                    dst_ref=dst(d),
                    send_sem=ssem.at[slot, d],
                    recv_sem=rsem.at[slot, d],
                    device_id=where(to),
                    device_id_type=MESH,
                )
            )
        for c in made:
            c.start()
        started.append(lambda: [c.wait_send() for c in made])
        return made

    started = []

    def arrived(made):
        for c in made:
            c.wait_recv()

    def whole(ref):
        return lambda to: ref

    def at(ref):
        return lambda d: ref.at[d]

    def at_rows(ref, rows):
        return lambda d: ref.at[d, rows]

    def from_y(k):
        return lax.rem(y + ny - k, ny)

    def from_z(k):
        return lax.rem(z + nz - k, nz)

    def cols_of(j):
        return pl.ds(pl.multiple_of(j * N, N), N)

    lane_low = iota((1, N), 1) < P_SIZE

    def lane_head(j):
        return 2 * j + jnp.where(lane_low, 0, 1)

    eye = iota((heads, heads), 0) == iota((heads, heads), 1)

    def column(row):
        return jnp.sum(
            jnp.where(eye, jnp.broadcast_to(row, (heads, heads)), 0.0), axis=1, keepdims=True
        )

    def row_of(col):
        return jnp.sum(
            jnp.where(eye, jnp.broadcast_to(col, (heads, heads)), 0.0), axis=0, keepdims=True
        )

    bias_raw = raw_ref[...] + column(bias_ref[...])
    delta = jnp.maximum(bias_raw, 0.0) + jnp.log1p(jnp.exp(-jnp.abs(bias_raw)))
    rate = jnp.exp(column(decay_ref[...]))
    skip_col = column(skip_ref[...])
    upto = (iota((toks, toks), 0) <= iota((toks, toks), 1)).astype(F32).astype(BF)
    a = nn3(-rate * delta, upto)
    a_end = a[:, toks - 1 : toks]
    dl_row[...] = delta
    stack = [a, jnp.exp(a), jnp.exp(a_end - a) * delta, delta]
    if 4 * heads < N:
        stack.append(jnp.zeros((N - 4 * heads, toks), F32))
    hi, mid, _ = split3(jnp.transpose(jnp.concatenate(stack, axis=0)))
    st_hi[...] = hi
    st_mid[...] = mid
    parts = [p.astype(F32) for p in split3(a)]
    for i in range(3):
        ahl_ref[i] = parts[i]
    tall = parts + [jnp.ones((8, toks), F32), jnp.zeros((N - 3 * heads - 8, toks), F32)]
    lhs_ref[...] = jnp.transpose(jnp.concatenate(tall, axis=0)).astype(BF)

    end_rows = jnp.broadcast_to(a_end, (heads, N))
    lg_buf[...] = jnp.zeros_like(lg_buf)
    for h in range(heads):
        lg_buf[h % ny, h // ny : h // ny + 1, :] = end_rows[h : h + 1, :]
    f_own[...] = jnp.exp(lg_buf[...])
    logs_y = exchange("y", at(lg_buf), at(lg_in))
    lg_in[0] = lg_buf[y]

    def put_heads(buf, j, both):
        for i in range(2):
            h = 2 * j + i
            rows = pl.ds(pl.multiple_of(lax.div(h, ny) * P_SIZE, P_SIZE), P_SIZE)
            buf[lax.rem(h, ny), rows, :] = both[i * P_SIZE : (i + 1) * P_SIZE, :]

    def take_heads(buf, j):
        got = []
        for i in range(2):
            h = 2 * j + i
            rows = pl.ds(pl.multiple_of(lax.div(h, ny) * P_SIZE, P_SIZE), P_SIZE)
            got.append(buf[from_y(lax.rem(h, ny)), rows, :])
        return jnp.concatenate(got, axis=0)

    per_chunk = nz // CHUNKS

    def loop(body, c, unroll=UNROLL):
        n = pairs // CHUNKS
        lax.fori_loop(c * n, (c + 1) * n, body, 0, unroll=min(n, unroll))

    def chunk_rows(c):
        return slice(c * per_chunk * P_SIZE, (c + 1) * per_chunk * P_SIZE)

    def first(j, _):
        cols = cols_of(j)
        place = jnp.concatenate(
            [(iota((N, N), 0) == q * heads + lane_head(j)).astype(F32) for q in (1, 2, 3)], axis=1
        ).astype(BF)
        wide = nn(st_hi[...], place) + nn(st_mid[...], place)
        e_ref[:, cols] = wide[:, :N]
        te_ref[:, cols] = wide[:, N : 2 * N]
        dl_ref[:, cols] = wide[:, 2 * N :]
        x = x_ref[:, cols].astype(F32)
        scaled = (x * wide[:, N : 2 * N]).astype(BF)
        xs_ref[:, cols] = scaled
        xd_ref[:, cols] = (x * wide[:, 2 * N :]).astype(BF)
        put_heads(s_buf, j, tn(scaled, w_ref[...]))
        return 0

    def skip_of(j):
        return jnp.sum(
            jnp.where(iota((heads, N), 0) == lane_head(j), skip_col, 0.0), axis=0, keepdims=True
        )

    def intra(j, _):
        cols = cols_of(j)
        xd = xd_ref[:, cols]
        made = []
        row = iota((N, toks), 0)
        for i in range(2):
            h = 2 * j + i
            rhs = jnp.where((row == h) | (row == heads + h) | (row == 2 * heads + h), 1.0, 0.0)
            for k in range(3):
                rhs = jnp.where(row == 3 * heads + k, -ahl_ref[k, pl.ds(h, 1), :], rhs)
            rhs = rhs.astype(BF)
            rhs_ref[h] = rhs
            gap = nn(lhs_ref[:half, :], rhs[:, :half])
            m = (rwm_ref[:half, :half] * jnp.exp(jnp.minimum(gap, 0.0))).astype(BF)
            top = nn(m, xd[:half])
            gap = nn(lhs_ref[half:, :], rhs)
            m = (rwm_ref[half:, :] * jnp.exp(jnp.minimum(gap, 0.0))).astype(BF)
            made.append(jnp.concatenate([top, nn(m, xd)], axis=0))
        yi = jnp.where(lane_low, made[0], made[1])
        ssd_ref[:, cols] = yi + skip_of(j) * x_ref[:, cols].astype(F32)
        gate = g_ref[:, cols].astype(F32)
        sig_ref[:, cols] = 1.0 / (1.0 + jnp.exp(-gate))
        return 0

    def rows_z(k):
        return slice(k * P_SIZE, (k + 1) * P_SIZE)

    def heads_of(c):
        return range(c * per_chunk, (c + 1) * per_chunk)

    def send_y(buf, into, c):
        rows = chunk_rows(c)
        made = exchange("y", at_rows(buf, rows), at_rows(into, rows))
        into[0, rows, :] = buf[y, rows, :]
        return made

    def to_owner(slot, buf, into, t):
        return pltpu.make_async_remote_copy(
            src_ref=buf.at[t],
            dst_ref=into.at[z],
            send_sem=ssem.at[slot, t],
            recv_sem=rsem.at[slot, z],
            device_id=along_z(t),
            device_id_type=MESH,
        )

    def from_sender(slot, buf, into, k):
        return pltpu.make_async_remote_copy(
            src_ref=buf.at[z],
            dst_ref=into.at[k],
            send_sem=ssem.at[slot, z],
            recv_sem=rsem.at[slot, k],
            device_id=along_z(k),
            device_id_type=MESH,
        )

    def to_row(slot, buf, into, d):
        to = lax.rem(z + d, nz)
        return pltpu.make_async_remote_copy(
            src_ref=buf.at[to],
            dst_ref=into.at[z],
            send_sem=ssem.at[slot, d],
            recv_sem=rsem.at[slot, z],
            device_id=along_z(to),
            device_id_type=MESH,
        )

    class Scan:
        def __init__(self, buf, into, back_buf, back_in):
            self.there, self.back = next(slots), next(slots)
            self.buf, self.into, self.back_buf, self.back_in = buf, into, back_buf, back_in

        def send(self, c):
            for t in heads_of(c):

                @pl.when(z != t)
                def _():
                    to_owner(self.there, self.buf, self.into, t).start()

                @pl.when(z == t)
                def _():
                    self.into[t] = self.buf[t]

        def scan(self, c, body):
            @pl.when(lax.div(z, per_chunk) == c)
            def _():
                for d in range(1, nz):
                    from_sender(self.there, self.buf, self.into, lax.rem(z + d, nz)).wait_recv()
                body()
                for d in range(1, nz):
                    to_row(self.back, self.back_buf, self.back_in, d).start()
                self.back_in[z] = self.back_buf[z]

        def wait(self, c):
            for t in heads_of(c):

                @pl.when(z != t)
                def _():
                    from_sender(self.back, self.back_buf, self.back_in, t).wait_recv()

        def sent(self):
            for t in range(nz):

                @pl.when(z != t)
                def _():
                    to_owner(self.there, self.buf, self.into, t).wait_send()

            for d in range(1, nz):
                to_row(self.back, self.back_buf, self.back_in, d).wait_send()

    forward = Scan(t_buf, t_in, zb_buf, zb_in)

    def compose(c):
        for j in heads_of(c):
            total = s_in[from_y(0), rows_z(j), :]
            for k in range(1, ny):
                total = f_ref[k, j : j + 1, :] * total + s_in[from_y(k), rows_z(j), :]
            t_buf[j] = total
        forward.send(c)

    def scan_forward():
        state = start_ref[...]
        for k in range(nz):
            zb_buf[k] = state
            state = fz_ref[k : k + 1, :] * state + t_in[k]
        fin_ref[...] = state

    def expand(c):
        forward.wait(c)
        for j in heads_of(c):
            state = zb_in[j]
            for k in range(ny):
                yb_buf[k, rows_z(j), :] = state
                if k < ny - 1:
                    state = f_ref[k, j : j + 1, :] * state + s_in[from_y(k), rows_z(j), :]
        return send_y(yb_buf, yb_in, c)

    def read(j, _):
        cols = cols_of(j)
        inc = take_heads(yb_in, j).astype(BF)
        ssd = ssd_ref[:, cols] + e_ref[:, cols] * nt(r_ref[...], inc)
        ssd_ref[:, cols] = ssd
        v = ssd * (g_ref[:, cols].astype(F32) * sig_ref[:, cols])
        v_ref[:, cols] = v
        acc_ref[0] += v * v
        acc_ref[1] += v * (og_ref[:, cols].astype(F32) * gain_ref[:, cols])
        return 0

    y_there, y_back = [], []
    for c in range(CHUNKS):
        loop(first, c)
        y_there.append(send_y(s_buf, s_in, c))
        if c == 1:
            arrived(logs_y)
            log_sum = jnp.zeros((8, N), F32)
            for k in range(ny):
                log_end = lg_in[from_y(k)]
                f_ref[k] = jnp.exp(log_end)
                log_sum = log_sum + log_end
            lr_buf[...] = log_sum
            logs_z = exchange("z", whole(lr_buf), at(lr_in))
            lr_in[0] = log_sum
    causal = iota((toks, toks), 0) >= iota((toks, toks), 1)
    rwm_ref[...] = jnp.where(causal, nt(r_ref[...], w_ref[...]), 0.0)
    rwt_ref[...] = jnp.where(
        iota((toks, toks), 0) <= iota((toks, toks), 1), nt(w_ref[...], r_ref[...]), 0.0
    )
    acc_ref[...] = jnp.zeros_like(acc_ref)
    arrived(y_there[0])
    compose(0)
    loop(intra, 0)
    arrived(y_there[1])
    compose(1)
    loop(intra, 1)
    arrived(y_there[2])
    compose(2)
    arrived(logs_z)
    for k in range(nz):
        fz_ref[k : k + 1, :] = jnp.exp(lr_in[from_z(k), pl.ds(z, 1), :])
    forward.scan(0, scan_forward)
    loop(intra, 2)
    arrived(y_there[3])
    compose(3)
    forward.scan(1, scan_forward)
    loop(intra, 3)
    forward.scan(2, scan_forward)
    y_back.append(expand(0))
    forward.scan(3, scan_forward)
    for c in range(1, 3):
        y_back.append(expand(c))
    arrived(y_back[0])
    loop(read, 0)
    y_back.append(expand(3))
    for c in range(1, CHUNKS):
        arrived(y_back[c])
        loop(read, c)
    tp_buf[0:1, :] = jnp.sum(jnp.transpose(acc_ref[0]), axis=0, keepdims=True)
    tp_buf[1:2, :] = jnp.sum(jnp.transpose(acc_ref[1]), axis=0, keepdims=True)
    tp_buf[2:, :] = jnp.zeros((6, toks), F32)
    tp_sums = exchange("t", whole(tp_buf), at(tp_in))
    tp_in[0] = tp_buf[...]
    arrived(tp_sums)
    both = tp_in[0]
    for k in range(1, ntp):
        both = both + tp_in[k]
    inverse = lax.rsqrt(both[0:1, :] / inner + EPS)
    slope = inverse * inverse * inverse * both[1:2, :] / inner
    invk_ref[0] = jnp.transpose(jnp.broadcast_to(inverse, (N, toks)))
    invk_ref[1] = jnp.transpose(jnp.broadcast_to(slope, (N, toks)))

    def back(j, _):
        cols = cols_of(j)
        sg = og_ref[:, cols].astype(F32) * gain_ref[:, cols]
        dv = invk_ref[0] * sg - v_ref[:, cols] * invk_ref[1]
        d = dv * (g_ref[:, cols].astype(F32) * sig_ref[:, cols])
        d_ref[:, cols] = d.astype(BF)
        de = (d * e_ref[:, cols]).astype(BF)
        de_ref[:, cols] = de
        put_heads(g_buf, j, tn(de, r_ref[...]))
        return 0

    rk_ref[...] = jnp.zeros_like(rk_ref)
    dwr_ref[...] = jnp.zeros_like(dwr_ref)
    drwt_ref[...] = jnp.zeros_like(drwt_ref)

    def gather_heads(j, prod):
        place = (
            iota((N, N), 1) == 2 * j + jnp.where(iota((N, N), 0) < P_SIZE, 0, 1)
        ).astype(F32).astype(BF)
        hi = prod.astype(BF)
        lo = (prod - hi.astype(F32)).astype(BF)
        return nn(hi, place) + nn(lo, place)

    def outs(j, _):
        cols = cols_of(j)
        og = og_ref[:, cols].astype(F32)
        gain = gain_ref[:, cols]
        v = v_ref[:, cols]
        ssd = ssd_ref[:, cols]
        vi = v * invk_ref[0]
        out_ref[:, cols] = (vi * gain).astype(BF)
        ny_buf[pl.ds(j, 1), :] = jnp.sum(og * vi, axis=0, keepdims=True)
        dv = invk_ref[0] * (og * gain) - v * invk_ref[1]
        gate = g_ref[:, cols].astype(F32)
        sig = sig_ref[:, cols]
        dg_ref[:, cols] = (dv * ssd * sig * (1.0 + gate * (1.0 - sig))).astype(BF)
        x = x_ref[:, cols].astype(F32)
        d = d_ref[:, cols].astype(F32)
        sk = jnp.sum(dv * (gate * sig) * x, axis=0, keepdims=True)
        sk_ref[pl.ds(2 * j, 1), :] = jnp.where(lane_low, sk, 0.0)
        sk_ref[pl.ds(2 * j + 1, 1), :] = jnp.where(lane_low, 0.0, sk)
        rk_ref[0] += gather_heads(j, d * (ssd - skip_of(j) * x))
        dwr_ref[1] += nn(de_ref[:, cols], take_heads(yb_in, j).astype(BF))
        return 0

    def intra_back(j, _):
        cols = cols_of(j)
        xd = xd_ref[:, cols]
        dp = d_ref[:, cols]
        made = []
        sums = None
        for i in range(2):
            h = 2 * j + i
            keep = lane_low if i == 0 else jnp.logical_not(lane_low)
            mine = jnp.where(keep, dp.astype(F32), 0.0).astype(BF)
            rhs = rhs_ref[h]
            decay = jnp.exp(jnp.minimum(-nn(lhs_ref[:half, :], rhs), 0.0))
            upper = nt(xd[:half], mine) * decay
            top = nn((rwt_ref[:half, :] * decay).astype(BF), dp)
            decay = jnp.exp(jnp.minimum(-nn(lhs_ref[half:, :], rhs[:, half:]), 0.0))
            lower = nt(xd[half:], mine[half:]) * decay
            low = nn((rwt_ref[half:, half:] * decay).astype(BF), dp[half:])
            made.append(jnp.concatenate([top, low], axis=0))
            sums = (upper, lower) if sums is None else (sums[0] + upper, sums[1] + lower)
        drwt_ref[:half, :] += sums[0]
        drwt_ref[half:, half:] += sums[1]
        unscaled = jnp.where(lane_low, made[0], made[1])
        v_ref[:, cols] = xd.astype(F32) * unscaled
        dxi_ref[:, cols] = unscaled * dl_ref[:, cols]
        return 0

    backward = Scan(u_buf, u_in, vb_buf, vb_in)

    def compose_back(c):
        for j in heads_of(c):
            total = g_in[from_y(ny - 1), rows_z(j), :]
            for k in range(ny - 2, -1, -1):
                total = f_ref[k, j : j + 1, :] * total + g_in[from_y(k), rows_z(j), :]
            u_buf[j] = total
        backward.send(c)

    def scan_back():
        state = jnp.zeros((P_SIZE, N), F32)
        for k in range(nz - 1, -1, -1):
            vb_buf[k] = state
            state = fz_ref[k : k + 1, :] * state + u_in[k]

    def expand_back(c):
        backward.wait(c)
        for j in heads_of(c):
            state = vb_in[j]
            for k in range(ny - 1, -1, -1):
                wb_buf[k, rows_z(j), :] = state
                if k > 0:
                    state = f_ref[k, j : j + 1, :] * state + g_in[from_y(k), rows_z(j), :]
        return send_y(wb_buf, wb_in, c)

    g_there, w_back = [], []
    for c in range(CHUNKS):
        loop(back, c)
        g_there.append(send_y(g_buf, g_in, c))
    loop(outs, 0)
    arrived(g_there[0])
    compose_back(0)
    loop(outs, 1)
    arrived(g_there[1])
    compose_back(1)
    loop(outs, 2)
    arrived(g_there[2])
    compose_back(2)
    loop(outs, 3)
    skip_sum = row_of(jnp.sum(sk_ref[...], axis=1, keepdims=True))
    ny_buf[pairs:, :] = jnp.zeros((ny_buf.shape[0] - pairs, N), F32)
    ny_buf[pairs : pairs + 1, :heads] = skip_sum
    sums_y = exchange("y", whole(ny_buf), at(ny_in))
    ny_in[0] = ny_buf[...]
    backward.scan(0, scan_back)
    loop(intra_back, 0)
    arrived(g_there[3])
    compose_back(3)
    backward.scan(1, scan_back)
    loop(intra_back, 1)
    backward.scan(2, scan_back)
    w_back.append(expand_back(0))
    loop(intra_back, 2)
    backward.scan(3, scan_back)
    for c in range(1, 3):
        w_back.append(expand_back(c))
    loop(intra_back, 3)
    w_back.append(expand_back(3))

    below = iota((toks, toks), 0) <= iota((toks, toks), 1)
    drwt = jnp.where(below, drwt_ref[...], 0.0).astype(BF)
    dr_in = tn(drwt, w_ref[...])
    dr_ref[...] = (dr_in.astype(BF).astype(F32) + dwr_ref[1].astype(BF).astype(F32)).astype(BF)
    dw_in = nn(drwt, r_ref[...])
    arrived(sums_y)
    total = ny_in[0]
    for k in range(1, ny):
        total = total + ny_in[k]
    nz_buf[...] = total
    sums_z = exchange("z", whole(nz_buf), at(nz_in))
    nz_in[0] = nz_buf[...]

    def last(j, _):
        cols = cols_of(j)
        later = take_heads(wb_in, j)
        inc = take_heads(yb_in, j)
        held = later * inc
        later = later.astype(BF)
        state_part = nt(w_ref[...], later) * te_ref[:, cols]
        intra_part = dxi_ref[:, cols]
        x = x_ref[:, cols].astype(F32)
        written = x * state_part
        rk_ref[1] += gather_heads(j, v_ref[:, cols] + written)
        written = jnp.sum(written, axis=0, keepdims=True)
        for i in range(2):
            h = 2 * j + i
            factor = f_own[lax.rem(h, ny), pl.ds(lax.div(h, ny), 1), :]
            kept = jnp.sum(held[i * P_SIZE : (i + 1) * P_SIZE], axis=0, keepdims=True)
            keep = lane_low if i == 0 else jnp.logical_not(lane_low)
            es_ref[pl.ds(h, 1), :] = factor * kept + jnp.where(keep, written, 0.0)
        direct = (d_ref[:, cols].astype(F32) * skip_of(j)).astype(BF).astype(F32)
        joined = (intra_part.astype(BF).astype(F32) + state_part.astype(BF).astype(F32)).astype(BF)
        dx_ref[:, cols] = (joined.astype(F32) + direct).astype(BF)
        dwr_ref[0] += nn(xs_ref[:, cols], later)
        return 0

    for c in range(CHUNKS):
        arrived(w_back[c])
        loop(last, c)
    dw_ref[...] = (dw_in.astype(BF).astype(F32) + dwr_ref[0].astype(BF).astype(F32)).astype(BF)

    k_rows = jnp.transpose(rk_ref[1])[:heads]
    d_log = jnp.transpose(rk_ref[0])[:heads] - k_rows
    end_sum = jnp.sum(es_ref[...], axis=1, keepdims=True)
    d_log = d_log + jnp.where(iota((heads, toks), 1) == toks - 1, end_sum, 0.0)
    from_on = (iota((toks, toks), 0) >= iota((toks, toks), 1)).astype(F32).astype(BF)
    d_inc = nn3(d_log, from_on)
    d_delta = k_rows / dl_row[...] - rate * d_inc
    again = raw_ref[...] + column(bias_ref[...])
    d_raw = d_delta * (1.0 / (1.0 + jnp.exp(-again)))
    dstep_ref[...] = d_raw
    ly_buf[...] = jnp.zeros_like(ly_buf)
    ly_buf[0:1, :heads] = row_of(jnp.sum(d_raw, axis=1, keepdims=True))
    ly_buf[1:2, :heads] = row_of(jnp.sum(d_inc * (-rate * dl_row[...]), axis=1, keepdims=True))
    late_y = exchange("y", whole(ly_buf), at(ly_in))
    ly_in[0] = ly_buf[...]
    arrived(late_y)
    total = ly_in[0]
    for k in range(1, ny):
        total = total + ly_in[k]
    lz_buf[...] = total
    late_z = exchange("z", whole(lz_buf), at(lz_in))
    lz_in[0] = lz_buf[...]
    arrived(sums_z)
    arrived(late_z)
    scale = 1.0 / math.sqrt(toks * ny * nz)
    total = nz_in[0]
    late = lz_in[0]
    for k in range(1, nz):
        total = total + nz_in[k]
        late = late + lz_in[k]
    for j in range(pairs):
        dnorm_ref[0:1, j * N : (j + 1) * N] = total[j : j + 1, :] * scale
    dheads_ref[0:2, :] = late[0:2, :heads] * scale
    dheads_ref[2:3, :] = total[pairs : pairs + 1, :heads] * scale
    forward.sent()
    backward.sent()
    for wait in started:
        wait()


def copy_kernel(*refs):
    n = (len(refs) - 1) // 2
    sem = refs[-1]
    made = [pltpu.make_async_copy(refs[i], refs[n + i], sem.at[i]) for i in range(n)]
    for c in made:
        c.start()
    for c in made:
        c.wait()


def solution(mesh):
    nctx, ntp = mesh.shape["ctx"], mesh.shape["tp"]
    ny, nz = NY, nctx // NY

    def on_device(
        inputs,
        gate_input,
        write_proj,
        read_proj,
        step_raw,
        step_bias,
        decay_log,
        skip_gain,
        norm_gain,
        start_state,
        out_grad,
    ):
        toks, cols = inputs.shape
        heads = step_raw.shape[0]
        pairs = heads // 2
        group = nz * P_SIZE
        f32, bf = F32, BF

        def v(shape, dtype=f32):
            return pltpu.VMEM(shape, dtype)

        scratch = [
            v((toks, N), bf),
            v((toks, N), bf),
            v((toks, N), bf),
            v((heads, N, toks), bf),
            v((3, heads, toks)),
            v((heads, toks)),
            v((toks, cols)),
            v((toks, cols)),
            v((toks, cols)),
            v((toks, cols), bf),
            v((toks, cols), bf),
            v((toks, cols)),
            v((toks, cols)),
            v((toks, cols)),
            v((toks, cols), bf),
            v((toks, cols), bf),
            v((toks, cols)),
            v((toks, toks)),
            v((toks, toks)),
            v((toks, toks)),
            v((2, toks, N)),
            v((2, toks, N)),
            v((2, toks, N)),
            v((2, toks, N)),
            v((heads, N)),
            v((heads, N)),
            v((ny, 8, N)),
            v((ny, 8, N)),
            v((8, N)),
            v((nz, 8, N)),
            v((ny, 8, N)),
            v((ny, 8, N)),
            v((8, N)),
            v((ny, group, N)),
            v((ny, group, N)),
            v((nz, P_SIZE, N)),
            v((nz, P_SIZE, N)),
            v((nz, P_SIZE, N)),
            v((nz, P_SIZE, N)),
            v((ny, group, N)),
            v((ny, group, N)),
            v((ny, group, N)),
            v((ny, group, N)),
            v((nz, P_SIZE, N)),
            v((nz, P_SIZE, N)),
            v((nz, P_SIZE, N)),
            v((nz, P_SIZE, N)),
            v((ny, group, N)),
            v((ny, group, N)),
            v((8, toks)),
            v((ntp, 8, toks)),
            v((pairs + 8, N)),
            v((ny, pairs + 8, N)),
            v((pairs + 8, N)),
            v((nz, pairs + 8, N)),
            v((8, N)),
            v((ny, 8, N)),
            v((8, N)),
            v((nz, 8, N)),
            pltpu.SemaphoreType.DMA((SLOTS, 8)),
            pltpu.SemaphoreType.DMA((SLOTS, 8)),
        ]
        vmem = pl.BlockSpec(memory_space=pltpu.VMEM)
        shapes = [
            jax.ShapeDtypeStruct((toks, cols), bf),
            jax.ShapeDtypeStruct((P_SIZE, N), f32),
            jax.ShapeDtypeStruct((toks, cols), bf),
            jax.ShapeDtypeStruct((toks, cols), bf),
            jax.ShapeDtypeStruct((toks, N), bf),
            jax.ShapeDtypeStruct((toks, N), bf),
            jax.ShapeDtypeStruct((heads, toks), f32),
            jax.ShapeDtypeStruct((3, heads), f32),
            jax.ShapeDtypeStruct((1, cols), f32),
        ]
        made = pl.pallas_call(
            functools.partial(kernel, ny, nz, ntp),
            out_shape=shapes,
            in_specs=[vmem] * 11,
            out_specs=[vmem] * 9,
            scratch_shapes=scratch,
            compiler_params=pltpu.CompilerParams(
                collective_id=0, has_side_effects=True, vmem_limit_bytes=60 * 2**20
            ),
        )(
            inputs,
            gate_input,
            write_proj,
            read_proj,
            step_raw,
            step_bias.reshape(1, heads),
            decay_log.reshape(1, heads),
            skip_gain.reshape(1, heads),
            norm_gain.reshape(1, cols),
            start_state.reshape(P_SIZE, N),
            out_grad,
        )
        anywhere = pl.BlockSpec(memory_space=pl.ANY)
        made = pl.pallas_call(
            copy_kernel,
            out_shape=shapes,
            in_specs=[vmem] * 9,
            out_specs=[anywhere] * 9,
            scratch_shapes=[pltpu.SemaphoreType.DMA((9,))],
        )(*made)
        output, final, dx, dg, dw, dr, dstep, dheads, dnorm = made
        return (
            output,
            final.reshape(1, 1, P_SIZE * N),
            dx,
            dg,
            dw,
            dr,
            dstep,
            dheads,
            dnorm.reshape(cols),
        )

    in_specs = (
        P("ctx", "tp"),
        P("ctx", "tp"),
        P("ctx", "tp"),
        P("ctx", "tp"),
        P("tp", "ctx"),
        P("tp"),
        P("tp"),
        P("tp"),
        P("tp"),
        P("tp", "ctx", None),
        P("ctx", "tp"),
    )
    out_specs = (
        P("ctx", "tp"),
        P("tp", "ctx", None),
        P("ctx", "tp"),
        P("ctx", "tp"),
        P("ctx", "tp"),
        P("ctx", "tp"),
        P("tp", "ctx"),
        P(None, "tp"),
        P("tp"),
    )
    return jax.shard_map(
        on_device, mesh=mesh, in_specs=in_specs, out_specs=out_specs, check_vma=False
    )
```

```python
import functools
import math

import jax
import jax.numpy as jnp
from jax import lax
from jax.experimental import pallas as pl
from jax.experimental.pallas import tpu as pltpu
from jax.sharding import PartitionSpec as P

P_SIZE = 64
N = 128
NY = 4
EPS = 1e-05
SLOTS = 11 + 4 * 4
CHUNKS = 4


def chunk_bounds(nz):
    return [0, 3, 5, 7, 8] if nz == 8 else [k * nz // CHUNKS for k in range(CHUNKS + 1)]


WINDOW = 9
F32 = jnp.float32
BF = jnp.bfloat16
MESH = pl.DeviceIdType.MESH


def contract(a, b, da, db):
    return lax.dot_general(a, b, (((da,), (db,)), ((), ())), preferred_element_type=F32)


def nn(a, b):
    return contract(a, b, 1, 0)


def nt(a, b):
    return contract(a, b, 1, 1)


def tn(a, b):
    return contract(a, b, 0, 0)


def split3(a):
    hi = a.astype(BF)
    rest = a - hi.astype(F32)
    mid = rest.astype(BF)
    return hi, mid, (rest - mid.astype(F32)).astype(BF)


def nn3(a, b):
    hi, mid, lo = split3(a)
    return nn(hi, b) + (nn(mid, b) + nn(lo, b))


def iota(shape, dim):
    return lax.broadcasted_iota(jnp.int32, shape, dim)


def kernel(
    ny,
    nz,
    ntp,
    ins,
    outs_hbm,
    held_in,
    held_out,
    io_sem,
    st_hi,
    st_mid,
    lhs_ref,
    rhs_ref,
    ahl_ref,
    dl_row,
    te_ref,
    e_ref,
    dl_ref,
    xs_ref,
    xd_ref,
    ssd_ref,
    sig_ref,
    v_ref,
    d_ref,
    de_ref,
    dxi_ref,
    rwm_ref,
    rwt_ref,
    drwt_ref,
    acc_ref,
    invk_ref,
    rk_ref,
    dwr_ref,
    sk_ref,
    es_ref,
    lg_buf,
    lg_in,
    lr_buf,
    lr_in,
    f_own,
    f_ref,
    fz_ref,
    s_buf,
    s_in,
    t_buf,
    t_in,
    zb_buf,
    zb_in,
    yb_buf,
    yb_in,
    g_buf,
    g_in,
    u_buf,
    u_in,
    vb_buf,
    vb_in,
    wb_buf,
    wb_in,
    tp_buf,
    tp_in,
    ny_buf,
    ny_in,
    nz_buf,
    nz_in,
    ly_buf,
    ly_in,
    lz_buf,
    lz_in,
    ssem,
    rsem,
):
    x_ref, g_ref, w_ref, r_ref, raw_ref, bias_ref, decay_ref, skip_ref, gain_ref = held_in[:9]
    start_ref, og_ref = held_in[9:]
    out_ref, fin_ref, dx_ref, dg_ref, dw_ref, dr_ref, dstep_ref, dheads_ref, dnorm_ref = held_out
    toks, cols_all = x_ref.shape
    loads = [pltpu.make_async_copy(ins[k], held_in[k], io_sem.at[0, k]) for k in range(11)]
    for k in (4, 5, 6, 7, 0, 2, 3, 1, 8, 9, 10):
        loads[k].start()

    def loaded(*which):
        for k in which:
            loads[k].wait()

    stores = [pltpu.make_async_copy(held_out[k], outs_hbm[k], io_sem.at[1, k]) for k in range(9)]

    def store(*which):
        for k in which:
            stores[k].start()

    heads = raw_ref.shape[0]
    pairs = heads // 2
    half = toks // 2
    inner = cols_all * ntp
    ctx = lax.axis_index("ctx")
    tp = lax.axis_index("tp")
    y = lax.rem(ctx, ny)
    z = lax.div(ctx, ny)

    def along_y(to):
        return {"ctx": z * ny + to}

    def along_z(to):
        return {"ctx": to * ny + y}

    def along_t(to):
        return {"tp": to}

    lines = {"y": (ny, y, along_y), "z": (nz, z, along_z), "t": (ntp, tp, along_t)}

    barrier = pltpu.get_barrier_semaphore()
    partners = 0
    for count, me, where in lines.values():
        for d in range(1, count):
            pl.semaphore_signal(
                barrier,
                inc=1,
                device_id=where(lax.rem(me + d, count)),
                device_id_type=MESH,
            )
            partners += 1
    slots = iter(range(SLOTS))

    def exchange(line, src, dst):
        slot = next(slots)
        count, me, where = lines[line]
        made = []
        for d in sorted(range(1, count), key=lambda d: -min(d, count - d)):
            to = lax.rem(me + d, count)
            made.append(
                pltpu.make_async_remote_copy(
                    src_ref=src(to),
                    dst_ref=dst(d),
                    send_sem=ssem.at[slot, d],
                    recv_sem=rsem.at[slot, d],
                    device_id=where(to),
                    device_id_type=MESH,
                )
            )
        for c in made:
            c.start()
        started.append(made)
        return made

    started, gone = [], []

    def sent(made):
        if not any(made is other for other in gone):
            gone.append(made)
            for c in made:
                c.wait_send()

    def arrived(made):
        for c in made:
            c.wait_recv()

    def whole(ref):
        return lambda to: ref

    def at(ref):
        return lambda d: ref.at[d]

    def at_rows(ref, rows):
        return lambda d: ref.at[d, rows]

    def from_y(k):
        return lax.rem(y + ny - k, ny)

    def from_z(k):
        return lax.rem(z + nz - k, nz)

    def cols_of(j):
        return pl.ds(pl.multiple_of(j * N, N), N)

    lane_low = iota((1, N), 1) < P_SIZE

    def lane_head(j):
        return 2 * j + jnp.where(lane_low, 0, 1)

    eye = iota((heads, heads), 0) == iota((heads, heads), 1)

    def column(row):
        return jnp.sum(
            jnp.where(eye, jnp.broadcast_to(row, (heads, heads)), 0.0), axis=1, keepdims=True
        )

    def row_of(col):
        return jnp.sum(
            jnp.where(eye, jnp.broadcast_to(col, (heads, heads)), 0.0), axis=0, keepdims=True
        )

    loaded(4, 5, 6, 7)
    bias_raw = raw_ref[...] + column(bias_ref[...])
    delta = jnp.maximum(bias_raw, 0.0) + jnp.log1p(jnp.exp(-jnp.abs(bias_raw)))
    rate = jnp.exp(column(decay_ref[...]))
    skip_col = column(skip_ref[...])
    upto = (iota((toks, toks), 0) <= iota((toks, toks), 1)).astype(F32).astype(BF)
    a = nn3(-rate * delta, upto)
    a_end = a[:, toks - 1 : toks]
    dl_row[...] = delta
    stack = [a, jnp.exp(a), jnp.exp(a_end - a) * delta, delta]
    if 4 * heads < N:
        stack.append(jnp.zeros((N - 4 * heads, toks), F32))
    hi, mid, _ = split3(jnp.transpose(jnp.concatenate(stack, axis=0)))
    st_hi[...] = hi
    st_mid[...] = mid
    parts = [p.astype(F32) for p in split3(a)]
    for i in range(3):
        ahl_ref[i] = parts[i]
    tall = parts + [jnp.ones((8, toks), F32), jnp.zeros((N - 3 * heads - 8, toks), F32)]
    lhs_ref[...] = jnp.transpose(jnp.concatenate(tall, axis=0)).astype(BF)

    end_rows = jnp.broadcast_to(a_end, (heads, N))
    lg_buf[...] = jnp.zeros_like(lg_buf)
    for h in range(heads):
        lg_buf[h % ny, h // ny : h // ny + 1, :] = end_rows[h : h + 1, :]
    f_own[...] = jnp.exp(lg_buf[...])

    def put_heads(buf, j, both):
        for i in range(2):
            h = 2 * j + i
            rows = pl.ds(pl.multiple_of(lax.div(h, ny) * P_SIZE, P_SIZE), P_SIZE)
            buf[lax.rem(h, ny), rows, :] = both[i * P_SIZE : (i + 1) * P_SIZE, :]

    def take_heads(buf, j):
        got = []
        for i in range(2):
            h = 2 * j + i
            rows = pl.ds(pl.multiple_of(lax.div(h, ny) * P_SIZE, P_SIZE), P_SIZE)
            got.append(buf[from_y(lax.rem(h, ny)), rows, :])
        return jnp.concatenate(got, axis=0)

    bounds = chunk_bounds(nz)

    def loop(body, c):
        lo, hi = bounds[c] * ny // 2, bounds[c + 1] * ny // 2
        lax.fori_loop(lo, hi, body, 0, unroll=hi - lo)

    def chunk_rows(c):
        return slice(bounds[c] * P_SIZE, bounds[c + 1] * P_SIZE)

    def first(j, _):
        cols = cols_of(j)
        place = jnp.concatenate(
            [(iota((N, N), 0) == q * heads + lane_head(j)).astype(F32) for q in (1, 2, 3)], axis=1
        ).astype(BF)
        wide = nn(st_hi[...], place) + nn(st_mid[...], place)
        e_ref[:, cols] = wide[:, :N]
        te_ref[:, cols] = wide[:, N : 2 * N]
        dl_ref[:, cols] = wide[:, 2 * N :]
        x = x_ref[:, cols].astype(F32)
        scaled = (x * wide[:, N : 2 * N]).astype(BF)
        xs_ref[:, cols] = scaled
        xd_ref[:, cols] = (x * wide[:, 2 * N :]).astype(BF)
        put_heads(s_buf, j, tn(scaled, w_ref[...]))
        return 0

    def skip_of(j):
        return jnp.sum(
            jnp.where(iota((heads, N), 0) == lane_head(j), skip_col, 0.0), axis=0, keepdims=True
        )

    def intra(j, _):
        cols = cols_of(j)
        xd = xd_ref[:, cols]
        made = []
        row = iota((N, toks), 0)
        for i in range(2):
            h = 2 * j + i
            rhs = jnp.where((row == h) | (row == heads + h) | (row == 2 * heads + h), 1.0, 0.0)
            for k in range(3):
                rhs = jnp.where(row == 3 * heads + k, -ahl_ref[k, pl.ds(h, 1), :], rhs)
            rhs = rhs.astype(BF)
            rhs_ref[h] = rhs
            gap = nn(lhs_ref[:half, :], rhs[:, :half])
            m = (rwm_ref[:half, :half] * jnp.exp(jnp.minimum(gap, 0.0))).astype(BF)
            top = nn(m, xd[:half])
            gap = nn(lhs_ref[half:, :], rhs)
            m = (rwm_ref[half:, :] * jnp.exp(jnp.minimum(gap, 0.0))).astype(BF)
            made.append(jnp.concatenate([top, nn(m, xd)], axis=0))
        yi = jnp.where(lane_low, made[0], made[1])
        ssd_ref[:, cols] = yi + skip_of(j) * x_ref[:, cols].astype(F32)
        gate = g_ref[:, cols].astype(F32)
        sig_ref[:, cols] = 1.0 / (1.0 + jnp.exp(-gate))
        return 0

    def rows_z(k):
        return slice(k * P_SIZE, (k + 1) * P_SIZE)

    def heads_of(c):
        return range(bounds[c], bounds[c + 1])

    def send_y(buf, into, c, before):
        if len(before) >= WINDOW:
            sent(before[-WINDOW])
        rows = chunk_rows(c)
        made = exchange("y", at_rows(buf, rows), at_rows(into, rows))
        into[0, rows, :] = buf[y, rows, :]
        before.append(made)

    def to_owner(slot, buf, into, t):
        return pltpu.make_async_remote_copy(
            src_ref=buf.at[t],
            dst_ref=into.at[z],
            send_sem=ssem.at[slot, t],
            recv_sem=rsem.at[slot, z],
            device_id=along_z(t),
            device_id_type=MESH,
        )

    def from_sender(slot, buf, into, k):
        return pltpu.make_async_remote_copy(
            src_ref=buf.at[z],
            dst_ref=into.at[k],
            send_sem=ssem.at[slot, z],
            recv_sem=rsem.at[slot, k],
            device_id=along_z(k),
            device_id_type=MESH,
        )

    def to_row(slot, buf, into, d):
        to = lax.rem(z + d, nz)
        return pltpu.make_async_remote_copy(
            src_ref=buf.at[to],
            dst_ref=into.at[z],
            send_sem=ssem.at[slot, d],
            recv_sem=rsem.at[slot, z],
            device_id=along_z(to),
            device_id_type=MESH,
        )

    class Scan:
        def __init__(self, buf, into, back_buf, back_in):
            self.there, self.back = next(slots), next(slots)
            self.buf, self.into, self.back_buf, self.back_in = buf, into, back_buf, back_in

        def send(self, c):
            for t in heads_of(c):

                @pl.when(z != t)
                def _():
                    to_owner(self.there, self.buf, self.into, t).start()

                @pl.when(z == t)
                def _():
                    self.into[t] = self.buf[t]

        def scan(self, c, body):
            @pl.when((z >= bounds[c]) & (z < bounds[c + 1]))
            def _():
                for d in range(1, nz):
                    from_sender(self.there, self.buf, self.into, lax.rem(z + d, nz)).wait_recv()
                body()
                for d in sorted(range(1, nz), key=lambda d: -min(d, nz - d)):
                    to_row(self.back, self.back_buf, self.back_in, d).start()
                self.back_in[z] = self.back_buf[z]

        def wait(self, c):
            for t in heads_of(c):

                @pl.when(z != t)
                def _():
                    from_sender(self.back, self.back_buf, self.back_in, t).wait_recv()

        def sent(self):
            for t in range(nz):

                @pl.when(z != t)
                def _():
                    to_owner(self.there, self.buf, self.into, t).wait_send()

            for d in range(1, nz):
                to_row(self.back, self.back_buf, self.back_in, d).wait_send()

    forward = Scan(t_buf, t_in, zb_buf, zb_in)

    def compose(c):
        for j in heads_of(c):
            total = s_in[from_y(0), rows_z(j), :]
            for k in range(1, ny):
                total = f_ref[k, j : j + 1, :] * total + s_in[from_y(k), rows_z(j), :]
            t_buf[j] = total
        forward.send(c)

    def scan_forward():
        state = start_ref[...]
        for k in range(nz):
            zb_buf[k] = state
            state = fz_ref[k : k + 1, :] * state + t_in[k]
        fin_ref[...] = state

    def expand(c):
        forward.wait(c)
        for j in heads_of(c):
            state = zb_in[j]
            for k in range(ny):
                yb_buf[k, rows_z(j), :] = state
                if k < ny - 1:
                    state = f_ref[k, j : j + 1, :] * state + s_in[from_y(k), rows_z(j), :]
        send_y(yb_buf, yb_in, c, y_back)

    def read(j, _):
        cols = cols_of(j)
        inc = take_heads(yb_in, j).astype(BF)
        ssd = ssd_ref[:, cols] + e_ref[:, cols] * nt(r_ref[...], inc)
        ssd_ref[:, cols] = ssd
        v = ssd * (g_ref[:, cols].astype(F32) * sig_ref[:, cols])
        v_ref[:, cols] = v
        acc_ref[0] += v * v
        acc_ref[1] += v * (og_ref[:, cols].astype(F32) * gain_ref[:, cols])
        return 0

    y_there, y_back = [], []
    loaded(0, 2, 3)
    loop(first, 0)
    pl.semaphore_wait(barrier, partners)
    logs_y = exchange("y", at(lg_buf), at(lg_in))
    lg_in[0] = lg_buf[y]
    send_y(s_buf, s_in, 0, y_there)
    for c in range(1, CHUNKS):
        loop(first, c)
        send_y(s_buf, s_in, c, y_there)
    causal = iota((toks, toks), 0) >= iota((toks, toks), 1)
    rwm_ref[...] = jnp.where(causal, nt(r_ref[...], w_ref[...]), 0.0)
    rwt_ref[...] = jnp.where(
        iota((toks, toks), 0) <= iota((toks, toks), 1), nt(w_ref[...], r_ref[...]), 0.0
    )
    acc_ref[...] = jnp.zeros_like(acc_ref)
    arrived(logs_y)
    log_sum = jnp.zeros((8, N), F32)
    for k in range(ny):
        log_end = lg_in[from_y(k)]
        f_ref[k] = jnp.exp(log_end)
        log_sum = log_sum + log_end
    lr_buf[...] = log_sum
    logs_z = exchange("z", whole(lr_buf), at(lr_in))
    lr_in[0] = log_sum
    loaded(1, 8, 9, 10)
    arrived(y_there[0])
    compose(0)
    loop(intra, 0)
    arrived(y_there[1])
    compose(1)
    loop(intra, 1)
    arrived(y_there[2])
    compose(2)
    arrived(logs_z)
    for k in range(nz):
        fz_ref[k : k + 1, :] = jnp.exp(lr_in[from_z(k), pl.ds(z, 1), :])
    forward.scan(0, scan_forward)
    loop(intra, 2)
    arrived(y_there[3])
    compose(3)
    forward.scan(1, scan_forward)
    loop(intra, 3)
    forward.scan(2, scan_forward)
    expand(0)
    forward.scan(3, scan_forward)
    store(1)
    for c in range(1, 3):
        expand(c)
    arrived(y_back[0])
    loop(read, 0)
    expand(3)
    for c in range(1, CHUNKS):
        arrived(y_back[c])
        loop(read, c)
    tp_buf[0:1, :] = jnp.sum(jnp.transpose(acc_ref[0]), axis=0, keepdims=True)
    tp_buf[1:2, :] = jnp.sum(jnp.transpose(acc_ref[1]), axis=0, keepdims=True)
    tp_buf[2:, :] = jnp.zeros((6, toks), F32)
    tp_sums = exchange("t", whole(tp_buf), at(tp_in))
    tp_in[0] = tp_buf[...]
    arrived(tp_sums)
    both = tp_in[0]
    for k in range(1, ntp):
        both = both + tp_in[k]
    inverse = lax.rsqrt(both[0:1, :] / inner + EPS)
    slope = inverse * inverse * inverse * both[1:2, :] / inner
    invk_ref[0] = jnp.transpose(jnp.broadcast_to(inverse, (N, toks)))
    invk_ref[1] = jnp.transpose(jnp.broadcast_to(slope, (N, toks)))

    def back(j, _):
        cols = cols_of(j)
        sg = og_ref[:, cols].astype(F32) * gain_ref[:, cols]
        dv = invk_ref[0] * sg - v_ref[:, cols] * invk_ref[1]
        d = dv * (g_ref[:, cols].astype(F32) * sig_ref[:, cols])
        d_ref[:, cols] = d.astype(BF)
        de = (d * e_ref[:, cols]).astype(BF)
        de_ref[:, cols] = de
        put_heads(g_buf, j, tn(de, r_ref[...]))
        return 0

    rk_ref[...] = jnp.zeros_like(rk_ref)
    dwr_ref[...] = jnp.zeros_like(dwr_ref)
    drwt_ref[...] = jnp.zeros_like(drwt_ref)

    def gather_heads(j, prod):
        place = (
            iota((N, N), 1) == 2 * j + jnp.where(iota((N, N), 0) < P_SIZE, 0, 1)
        ).astype(F32).astype(BF)
        hi = prod.astype(BF)
        lo = (prod - hi.astype(F32)).astype(BF)
        return nn(hi, place) + nn(lo, place)

    def outs(j, _):
        cols = cols_of(j)
        og = og_ref[:, cols].astype(F32)
        gain = gain_ref[:, cols]
        v = v_ref[:, cols]
        ssd = ssd_ref[:, cols]
        vi = v * invk_ref[0]
        out_ref[:, cols] = (vi * gain).astype(BF)
        ny_buf[pl.ds(j, 1), :] = jnp.sum(og * vi, axis=0, keepdims=True)
        dv = invk_ref[0] * (og * gain) - v * invk_ref[1]
        gate = g_ref[:, cols].astype(F32)
        sig = sig_ref[:, cols]
        dg_ref[:, cols] = (dv * ssd * sig * (1.0 + gate * (1.0 - sig))).astype(BF)
        x = x_ref[:, cols].astype(F32)
        d = d_ref[:, cols].astype(F32)
        sk = jnp.sum(dv * (gate * sig) * x, axis=0, keepdims=True)
        sk_ref[pl.ds(2 * j, 1), :] = jnp.where(lane_low, sk, 0.0)
        sk_ref[pl.ds(2 * j + 1, 1), :] = jnp.where(lane_low, 0.0, sk)
        rk_ref[0] += gather_heads(j, d * (ssd - skip_of(j) * x))
        dwr_ref[1] += nn(de_ref[:, cols], take_heads(yb_in, j).astype(BF))
        return 0

    def intra_back(j, _):
        cols = cols_of(j)
        xd = xd_ref[:, cols]
        dp = d_ref[:, cols]
        made = []
        sums = None
        for i in range(2):
            h = 2 * j + i
            keep = lane_low if i == 0 else jnp.logical_not(lane_low)
            mine = jnp.where(keep, dp.astype(F32), 0.0).astype(BF)
            rhs = rhs_ref[h]
            decay = jnp.exp(jnp.minimum(-nn(lhs_ref[:half, :], rhs), 0.0))
            upper = nt(xd[:half], mine) * decay
            top = nn((rwt_ref[:half, :] * decay).astype(BF), dp)
            decay = jnp.exp(jnp.minimum(-nn(lhs_ref[half:, :], rhs[:, half:]), 0.0))
            lower = nt(xd[half:], mine[half:]) * decay
            low = nn((rwt_ref[half:, half:] * decay).astype(BF), dp[half:])
            made.append(jnp.concatenate([top, low], axis=0))
            sums = (upper, lower) if sums is None else (sums[0] + upper, sums[1] + lower)
        drwt_ref[:half, :] += sums[0]
        drwt_ref[half:, half:] += sums[1]
        unscaled = jnp.where(lane_low, made[0], made[1])
        v_ref[:, cols] = xd.astype(F32) * unscaled
        dxi_ref[:, cols] = unscaled * dl_ref[:, cols]
        return 0

    backward = Scan(u_buf, u_in, vb_buf, vb_in)

    def compose_back(c):
        for j in heads_of(c):
            total = g_in[from_y(ny - 1), rows_z(j), :]
            for k in range(ny - 2, -1, -1):
                total = f_ref[k, j : j + 1, :] * total + g_in[from_y(k), rows_z(j), :]
            u_buf[j] = total
        backward.send(c)

    def scan_back():
        state = jnp.zeros((P_SIZE, N), F32)
        for k in range(nz - 1, -1, -1):
            vb_buf[k] = state
            state = fz_ref[k : k + 1, :] * state + u_in[k]

    def expand_back(c):
        backward.wait(c)
        for j in heads_of(c):
            state = vb_in[j]
            for k in range(ny - 1, -1, -1):
                wb_buf[k, rows_z(j), :] = state
                if k > 0:
                    state = f_ref[k, j : j + 1, :] * state + g_in[from_y(k), rows_z(j), :]
        send_y(wb_buf, wb_in, c, w_back)

    g_there, w_back = [], []
    for c in range(CHUNKS):
        loop(back, c)
        send_y(g_buf, g_in, c, g_there)
    loop(outs, 0)
    arrived(g_there[0])
    compose_back(0)
    loop(outs, 1)
    arrived(g_there[1])
    compose_back(1)
    loop(outs, 2)
    arrived(g_there[2])
    compose_back(2)
    loop(outs, 3)
    store(0, 3)
    skip_sum = row_of(jnp.sum(sk_ref[...], axis=1, keepdims=True))
    ny_buf[pairs:, :] = jnp.zeros((ny_buf.shape[0] - pairs, N), F32)
    ny_buf[pairs : pairs + 1, :heads] = skip_sum
    sums_y = exchange("y", whole(ny_buf), at(ny_in))
    ny_in[0] = ny_buf[...]
    backward.scan(0, scan_back)
    loop(intra_back, 0)
    arrived(g_there[3])
    compose_back(3)
    backward.scan(1, scan_back)
    loop(intra_back, 1)
    backward.scan(2, scan_back)
    expand_back(0)
    loop(intra_back, 2)
    backward.scan(3, scan_back)
    for c in range(1, 3):
        expand_back(c)
    loop(intra_back, 3)
    expand_back(3)

    below = iota((toks, toks), 0) <= iota((toks, toks), 1)
    drwt = jnp.where(below, drwt_ref[...], 0.0).astype(BF)
    dr_in = tn(drwt, w_ref[...])
    dr_ref[...] = (dr_in.astype(BF).astype(F32) + dwr_ref[1].astype(BF).astype(F32)).astype(BF)
    store(5)
    dw_in = nn(drwt, r_ref[...])
    arrived(sums_y)
    total = ny_in[0]
    for k in range(1, ny):
        total = total + ny_in[k]
    nz_buf[...] = total
    sums_z = exchange("z", whole(nz_buf), at(nz_in))
    nz_in[0] = nz_buf[...]

    def last(j, _):
        cols = cols_of(j)
        later = take_heads(wb_in, j)
        inc = take_heads(yb_in, j)
        held = later * inc
        later = later.astype(BF)
        state_part = nt(w_ref[...], later) * te_ref[:, cols]
        x = x_ref[:, cols].astype(F32)
        written = x * state_part
        rk_ref[1] += gather_heads(j, v_ref[:, cols] + written)
        written = jnp.sum(written, axis=0, keepdims=True)
        for i in range(2):
            h = 2 * j + i
            factor = f_own[lax.rem(h, ny), pl.ds(lax.div(h, ny), 1), :]
            kept = jnp.sum(held[i * P_SIZE : (i + 1) * P_SIZE], axis=0, keepdims=True)
            keep = lane_low if i == 0 else jnp.logical_not(lane_low)
            es_ref[pl.ds(h, 1), :] = factor * kept + jnp.where(keep, written, 0.0)
        te_ref[:, cols] = state_part
        return 0

    def inputs_back(j, _):
        cols = cols_of(j)
        state_part = te_ref[:, cols]
        intra_part = dxi_ref[:, cols]
        direct = (d_ref[:, cols].astype(F32) * skip_of(j)).astype(BF).astype(F32)
        joined = (intra_part.astype(BF).astype(F32) + state_part.astype(BF).astype(F32)).astype(BF)
        dx_ref[:, cols] = (joined.astype(F32) + direct).astype(BF)
        dwr_ref[0] += nn(xs_ref[:, cols], take_heads(wb_in, j).astype(BF))
        return 0

    for c in range(CHUNKS):
        arrived(w_back[c])
        loop(last, c)
        if c < CHUNKS - 2:
            loop(inputs_back, c)

    k_rows = jnp.transpose(rk_ref[1])[:heads]
    d_log = jnp.transpose(rk_ref[0])[:heads] - k_rows
    end_sum = jnp.sum(es_ref[...], axis=1, keepdims=True)
    d_log = d_log + jnp.where(iota((heads, toks), 1) == toks - 1, end_sum, 0.0)
    from_on = (iota((toks, toks), 0) >= iota((toks, toks), 1)).astype(F32).astype(BF)
    d_inc = nn3(d_log, from_on)
    d_delta = k_rows / dl_row[...] - rate * d_inc
    again = raw_ref[...] + column(bias_ref[...])
    d_raw = d_delta * (1.0 / (1.0 + jnp.exp(-again)))
    dstep_ref[...] = d_raw
    ly_buf[...] = jnp.zeros_like(ly_buf)
    ly_buf[0:1, :heads] = row_of(jnp.sum(d_raw, axis=1, keepdims=True))
    ly_buf[1:2, :heads] = row_of(jnp.sum(d_inc * (-rate * dl_row[...]), axis=1, keepdims=True))
    late_y = exchange("y", whole(ly_buf), at(ly_in))
    ly_in[0] = ly_buf[...]
    for c in range(CHUNKS - 2, CHUNKS):
        loop(inputs_back, c)
    store(2, 6)
    dw_ref[...] = (dw_in.astype(BF).astype(F32) + dwr_ref[0].astype(BF).astype(F32)).astype(BF)
    store(4)
    arrived(late_y)
    total = ly_in[0]
    for k in range(1, ny):
        total = total + ly_in[k]
    lz_buf[...] = total
    late_z = exchange("z", whole(lz_buf), at(lz_in))
    lz_in[0] = lz_buf[...]
    arrived(sums_z)
    arrived(late_z)
    scale = 1.0 / math.sqrt(toks * ny * nz)
    total = nz_in[0]
    late = lz_in[0]
    for k in range(1, nz):
        total = total + nz_in[k]
        late = late + lz_in[k]
    for j in range(pairs):
        dnorm_ref[0:1, j * N : (j + 1) * N] = total[j : j + 1, :] * scale
    dheads_ref[0:2, :] = late[0:2, :heads] * scale
    dheads_ref[2:3, :] = total[pairs : pairs + 1, :heads] * scale
    store(7, 8)
    forward.sent()
    backward.sent()
    for made in started:
        sent(made)
    for made in stores:
        made.wait()


def copy_kernel(n, *refs):
    sources, places, held, sem = refs[:n], refs[n : 2 * n], refs[2 * n : 3 * n], refs[-1]
    made = []
    for i in range(n):
        load = pltpu.make_async_copy(sources[i], held[i], sem.at[0, i])
        load.start()
        made.append((load, pltpu.make_async_copy(held[i], places[i], sem.at[1, i])))
    for load, store in made:
        load.wait()
        store.start()
    for _, store in made:
        store.wait()


def solution(mesh):
    nctx, ntp = mesh.shape["ctx"], mesh.shape["tp"]
    ny, nz = NY, nctx // NY

    def on_device(
        inputs,
        gate_input,
        write_proj,
        read_proj,
        step_raw,
        step_bias,
        decay_log,
        skip_gain,
        norm_gain,
        start_state,
        out_grad,
    ):
        toks, cols = inputs.shape
        heads = step_raw.shape[0]
        pairs = heads // 2
        group = nz * P_SIZE
        f32, bf = F32, BF

        def v(shape, dtype=f32):
            return pltpu.VMEM(shape, dtype)

        scratch = [
            pltpu.SemaphoreType.DMA((2, 11)),
            v((toks, N), bf),
            v((toks, N), bf),
            v((toks, N), bf),
            v((heads, N, toks), bf),
            v((3, heads, toks)),
            v((heads, toks)),
            v((toks, cols)),
            v((toks, cols)),
            v((toks, cols)),
            v((toks, cols), bf),
            v((toks, cols), bf),
            v((toks, cols)),
            v((toks, cols)),
            v((toks, cols)),
            v((toks, cols), bf),
            v((toks, cols), bf),
            v((toks, cols)),
            v((toks, toks)),
            v((toks, toks)),
            v((toks, toks)),
            v((2, toks, N)),
            v((2, toks, N)),
            v((2, toks, N)),
            v((2, toks, N)),
            v((heads, N)),
            v((heads, N)),
            v((ny, 8, N)),
            v((ny, 8, N)),
            v((8, N)),
            v((nz, 8, N)),
            v((ny, 8, N)),
            v((ny, 8, N)),
            v((8, N)),
            v((ny, group, N)),
            v((ny, group, N)),
            v((nz, P_SIZE, N)),
            v((nz, P_SIZE, N)),
            v((nz, P_SIZE, N)),
            v((nz, P_SIZE, N)),
            v((ny, group, N)),
            v((ny, group, N)),
            v((ny, group, N)),
            v((ny, group, N)),
            v((nz, P_SIZE, N)),
            v((nz, P_SIZE, N)),
            v((nz, P_SIZE, N)),
            v((nz, P_SIZE, N)),
            v((ny, group, N)),
            v((ny, group, N)),
            v((8, toks)),
            v((ntp, 8, toks)),
            v((pairs + 8, N)),
            v((ny, pairs + 8, N)),
            v((pairs + 8, N)),
            v((nz, pairs + 8, N)),
            v((8, N)),
            v((ny, 8, N)),
            v((8, N)),
            v((nz, 8, N)),
            pltpu.SemaphoreType.DMA((SLOTS, 8)),
            pltpu.SemaphoreType.DMA((SLOTS, 8)),
        ]
        anywhere = pl.BlockSpec(memory_space=pl.ANY)
        shapes = [
            jax.ShapeDtypeStruct((toks, cols), bf),
            jax.ShapeDtypeStruct((P_SIZE, N), f32),
            jax.ShapeDtypeStruct((toks, cols), bf),
            jax.ShapeDtypeStruct((toks, cols), bf),
            jax.ShapeDtypeStruct((toks, N), bf),
            jax.ShapeDtypeStruct((toks, N), bf),
            jax.ShapeDtypeStruct((heads, toks), f32),
            jax.ShapeDtypeStruct((3, heads), f32),
            jax.ShapeDtypeStruct((1, cols), f32),
        ]
        operands = (
            inputs,
            gate_input,
            write_proj,
            read_proj,
            step_raw,
            step_bias.reshape(1, heads),
            decay_log.reshape(1, heads),
            skip_gain.reshape(1, heads),
            norm_gain.reshape(1, cols),
            start_state.reshape(P_SIZE, N),
            out_grad,
        )
        held_in = [v(a.shape, a.dtype) for a in operands]
        held_out = [v(a.shape, a.dtype) for a in shapes]

        def whole_kernel(*refs):
            kernel(ny, nz, ntp, refs[:11], refs[11:20], refs[20:31], refs[31:40], *refs[40:])

        made = pl.pallas_call(
            whole_kernel,
            out_shape=shapes,
            in_specs=[anywhere] * 11,
            out_specs=[anywhere] * 9,
            scratch_shapes=held_in + held_out + scratch,
            compiler_params=pltpu.CompilerParams(
                collective_id=0, has_side_effects=True, vmem_limit_bytes=60 * 2**20
            ),
        )(*operands)
        made = pl.pallas_call(
            functools.partial(copy_kernel, 9),
            out_shape=shapes,
            in_specs=[anywhere] * 9,
            out_specs=[anywhere] * 9,
            scratch_shapes=[v(a.shape, a.dtype) for a in shapes]
            + [pltpu.SemaphoreType.DMA((2, 9))],
        )(*made)
        output, final, dx, dg, dw, dr, dstep, dheads, dnorm = made
        return (
            output,
            final.reshape(1, 1, P_SIZE * N),
            dx,
            dg,
            dw,
            dr,
            dstep,
            dheads,
            dnorm.reshape(cols),
        )

    in_specs = (
        P("ctx", "tp"),
        P("ctx", "tp"),
        P("ctx", "tp"),
        P("ctx", "tp"),
        P("tp", "ctx"),
        P("tp"),
        P("tp"),
        P("tp"),
        P("tp"),
        P("tp", "ctx", None),
        P("ctx", "tp"),
    )
    out_specs = (
        P("ctx", "tp"),
        P("tp", "ctx", None),
        P("ctx", "tp"),
        P("ctx", "tp"),
        P("ctx", "tp"),
        P("ctx", "tp"),
        P("tp", "ctx"),
        P(None, "tp"),
        P("tp"),
    )
    return jax.shard_map(
        on_device, mesh=mesh, in_specs=in_specs, out_specs=out_specs, check_vma=False
    )
```

```python
import functools
import math

import jax
import jax.numpy as jnp
from jax import lax
from jax.experimental import pallas as pl
from jax.experimental.pallas import tpu as pltpu
from jax.sharding import PartitionSpec as P

P_SIZE = 64
N = 128
NY = 4
EPS = 1e-05
SLOTS = 11 + 4 * 4
CHUNKS = 4


def chunk_bounds(nz):
    return [0, 1, 4, 7, 8] if nz == 8 else [k * nz // CHUNKS for k in range(CHUNKS + 1)]


WINDOW = 9
F32 = jnp.float32
BF = jnp.bfloat16
MESH = pl.DeviceIdType.MESH


def contract(a, b, da, db):
    return lax.dot_general(a, b, (((da,), (db,)), ((), ())), preferred_element_type=F32)


def nn(a, b):
    return contract(a, b, 1, 0)


def nt(a, b):
    return contract(a, b, 1, 1)


def tn(a, b):
    return contract(a, b, 0, 0)


def split3(a):
    hi = a.astype(BF)
    rest = a - hi.astype(F32)
    mid = rest.astype(BF)
    return hi, mid, (rest - mid.astype(F32)).astype(BF)


def nn3(a, b):
    hi, mid, lo = split3(a)
    return nn(hi, b) + (nn(mid, b) + nn(lo, b))


def iota(shape, dim):
    return lax.broadcasted_iota(jnp.int32, shape, dim)


def kernel(
    ny,
    nz,
    ntp,
    ins,
    outs_hbm,
    held_in,
    held_out,
    io_sem,
    st_hi,
    st_mid,
    lhs_ref,
    rhs_ref,
    ahl_ref,
    dl_row,
    te_ref,
    e_ref,
    dl_ref,
    xs_ref,
    xd_ref,
    ssd_ref,
    sig_ref,
    v_ref,
    d_ref,
    de_ref,
    dxi_ref,
    rwm_ref,
    rwt_ref,
    drwt_ref,
    acc_ref,
    invk_ref,
    rk_ref,
    dwr_ref,
    sk_ref,
    es_ref,
    lg_buf,
    lg_in,
    lr_buf,
    lr_in,
    f_own,
    f_ref,
    fz_ref,
    s_buf,
    s_in,
    t_buf,
    t_in,
    zb_buf,
    zb_in,
    yb_buf,
    yb_in,
    g_buf,
    g_in,
    u_buf,
    u_in,
    vb_buf,
    vb_in,
    wb_buf,
    wb_in,
    tp_buf,
    tp_in,
    ny_buf,
    ny_in,
    nz_buf,
    nz_in,
    ly_buf,
    ly_in,
    lz_buf,
    lz_in,
    ssem,
    rsem,
):
    x_ref, g_ref, w_ref, r_ref, raw_ref, bias_ref, decay_ref, skip_ref, gain_ref = held_in[:9]
    start_ref, og_ref = held_in[9:]
    out_ref, fin_ref, dx_ref, dg_ref, dw_ref, dr_ref, dstep_ref, dheads_ref, dnorm_ref = held_out
    toks, cols_all = x_ref.shape
    loads = [pltpu.make_async_copy(ins[k], held_in[k], io_sem.at[0, k]) for k in range(11)]
    for k in (4, 5, 6, 7, 0, 2, 3, 1, 8, 9, 10):
        loads[k].start()

    def loaded(*which):
        for k in which:
            loads[k].wait()

    stores = [pltpu.make_async_copy(held_out[k], outs_hbm[k], io_sem.at[1, k]) for k in range(9)]

    def store(*which):
        for k in which:
            stores[k].start()

    heads = raw_ref.shape[0]
    pairs = heads // 2
    half = toks // 2
    inner = cols_all * ntp
    ctx = lax.axis_index("ctx")
    tp = lax.axis_index("tp")
    y = lax.rem(ctx, ny)
    z = lax.div(ctx, ny)

    def along_y(to):
        return {"ctx": z * ny + to}

    def along_z(to):
        return {"ctx": to * ny + y}

    def along_t(to):
        return {"tp": to}

    lines = {"y": (ny, y, along_y), "z": (nz, z, along_z), "t": (ntp, tp, along_t)}

    barrier = pltpu.get_barrier_semaphore()
    partners = 0
    for count, me, where in lines.values():
        for d in range(1, count):
            pl.semaphore_signal(
                barrier,
                inc=1,
                device_id=where(lax.rem(me + d, count)),
                device_id_type=MESH,
            )
            partners += 1
    slots = iter(range(SLOTS))

    def exchange(line, src, dst):
        slot = next(slots)
        count, me, where = lines[line]
        made = []
        for d in sorted(range(1, count), key=lambda d: -min(d, count - d)):
            to = lax.rem(me + d, count)
            made.append(
                pltpu.make_async_remote_copy(
                    src_ref=src(to),
                    dst_ref=dst(d),
                    send_sem=ssem.at[slot, d],
                    recv_sem=rsem.at[slot, d],
                    device_id=where(to),
                    device_id_type=MESH,
                )
            )
        for c in made:
            c.start()
        started.append(made)
        return made

    started, gone = [], []

    def sent(made):
        if not any(made is other for other in gone):
            gone.append(made)
            for c in made:
                c.wait_send()

    def arrived(made):
        for c in made:
            c.wait_recv()

    def whole(ref):
        return lambda to: ref

    def at(ref):
        return lambda d: ref.at[d]

    def at_rows(ref, rows):
        return lambda d: ref.at[d, rows]

    def from_y(k):
        return lax.rem(y + ny - k, ny)

    def from_z(k):
        return lax.rem(z + nz - k, nz)

    def cols_of(j):
        return pl.ds(pl.multiple_of(j * N, N), N)

    lane_low = iota((1, N), 1) < P_SIZE

    def lane_head(j):
        return 2 * j + jnp.where(lane_low, 0, 1)

    eye = iota((heads, heads), 0) == iota((heads, heads), 1)

    def column(row):
        return jnp.sum(
            jnp.where(eye, jnp.broadcast_to(row, (heads, heads)), 0.0), axis=1, keepdims=True
        )

    def row_of(col):
        return jnp.sum(
            jnp.where(eye, jnp.broadcast_to(col, (heads, heads)), 0.0), axis=0, keepdims=True
        )

    loaded(4, 5, 6, 7)
    bias_raw = raw_ref[...] + column(bias_ref[...])
    delta = jnp.maximum(bias_raw, 0.0) + jnp.log1p(jnp.exp(-jnp.abs(bias_raw)))
    rate = jnp.exp(column(decay_ref[...]))
    skip_col = column(skip_ref[...])
    upto = (iota((toks, toks), 0) <= iota((toks, toks), 1)).astype(F32).astype(BF)
    a = nn3(-rate * delta, upto)
    a_end = a[:, toks - 1 : toks]
    dl_row[...] = delta
    stack = [a, jnp.exp(a), jnp.exp(a_end - a) * delta, delta]
    if 4 * heads < N:
        stack.append(jnp.zeros((N - 4 * heads, toks), F32))
    hi, mid, _ = split3(jnp.transpose(jnp.concatenate(stack, axis=0)))
    st_hi[...] = hi
    st_mid[...] = mid
    parts = [p.astype(F32) for p in split3(a)]
    for i in range(3):
        ahl_ref[i] = parts[i]
    tall = parts + [jnp.ones((8, toks), F32), jnp.zeros((N - 3 * heads - 8, toks), F32)]
    lhs_ref[...] = jnp.transpose(jnp.concatenate(tall, axis=0)).astype(BF)

    end_rows = jnp.broadcast_to(a_end, (heads, N))
    lg_buf[...] = jnp.zeros_like(lg_buf)
    for h in range(heads):
        lg_buf[h % ny, h // ny : h // ny + 1, :] = end_rows[h : h + 1, :]
    f_own[...] = jnp.exp(lg_buf[...])

    def put_heads(buf, j, both):
        for i in range(2):
            h = 2 * j + i
            rows = pl.ds(pl.multiple_of(lax.div(h, ny) * P_SIZE, P_SIZE), P_SIZE)
            buf[lax.rem(h, ny), rows, :] = both[i * P_SIZE : (i + 1) * P_SIZE, :]

    def take_heads(buf, j):
        got = []
        for i in range(2):
            h = 2 * j + i
            rows = pl.ds(pl.multiple_of(lax.div(h, ny) * P_SIZE, P_SIZE), P_SIZE)
            got.append(buf[from_y(lax.rem(h, ny)), rows, :])
        return jnp.concatenate(got, axis=0)

    bounds = chunk_bounds(nz)

    def loop(body, c):
        lo, hi = bounds[c] * ny // 2, bounds[c + 1] * ny // 2
        lax.fori_loop(lo, hi, body, 0, unroll=hi - lo)

    def chunk_rows(c):
        return slice(bounds[c] * P_SIZE, bounds[c + 1] * P_SIZE)

    def first(j, _):
        cols = cols_of(j)
        place = jnp.concatenate(
            [(iota((N, N), 0) == q * heads + lane_head(j)).astype(F32) for q in (1, 2, 3)], axis=1
        ).astype(BF)
        wide = nn(st_hi[...], place) + nn(st_mid[...], place)
        e_ref[:, cols] = wide[:, :N]
        te_ref[:, cols] = wide[:, N : 2 * N]
        dl_ref[:, cols] = wide[:, 2 * N :]
        x = x_ref[:, cols].astype(F32)
        scaled = (x * wide[:, N : 2 * N]).astype(BF)
        xs_ref[:, cols] = scaled
        xd_ref[:, cols] = (x * wide[:, 2 * N :]).astype(BF)
        put_heads(s_buf, j, tn(scaled, w_ref[...]))
        return 0

    def skip_of(j):
        return jnp.sum(
            jnp.where(iota((heads, N), 0) == lane_head(j), skip_col, 0.0), axis=0, keepdims=True
        )

    def intra(j, _):
        cols = cols_of(j)
        xd = xd_ref[:, cols]
        made = []
        row = iota((N, toks), 0)
        for i in range(2):
            h = 2 * j + i
            rhs = jnp.where((row == h) | (row == heads + h) | (row == 2 * heads + h), 1.0, 0.0)
            for k in range(3):
                rhs = jnp.where(row == 3 * heads + k, -ahl_ref[k, pl.ds(h, 1), :], rhs)
            rhs = rhs.astype(BF)
            rhs_ref[h] = rhs
            gap = nn(lhs_ref[:half, :], rhs[:, :half])
            m = (rwm_ref[:half, :half] * jnp.exp(jnp.minimum(gap, 0.0))).astype(BF)
            top = nn(m, xd[:half])
            gap = nn(lhs_ref[half:, :], rhs)
            m = (rwm_ref[half:, :] * jnp.exp(jnp.minimum(gap, 0.0))).astype(BF)
            made.append(jnp.concatenate([top, nn(m, xd)], axis=0))
        yi = jnp.where(lane_low, made[0], made[1])
        ssd_ref[:, cols] = yi + skip_of(j) * x_ref[:, cols].astype(F32)
        gate = g_ref[:, cols].astype(F32)
        sig_ref[:, cols] = 1.0 / (1.0 + jnp.exp(-gate))
        return 0

    def rows_z(k):
        return slice(k * P_SIZE, (k + 1) * P_SIZE)

    def heads_of(c):
        return range(bounds[c], bounds[c + 1])

    def send_y(buf, into, c, before):
        if len(before) >= WINDOW:
            sent(before[-WINDOW])
        rows = chunk_rows(c)
        made = exchange("y", at_rows(buf, rows), at_rows(into, rows))
        into[0, rows, :] = buf[y, rows, :]
        before.append(made)

    def to_owner(slot, buf, into, t):
        return pltpu.make_async_remote_copy(
            src_ref=buf.at[t],
            dst_ref=into.at[z],
            send_sem=ssem.at[slot, t],
            recv_sem=rsem.at[slot, z],
            device_id=along_z(t),
            device_id_type=MESH,
        )

    def from_sender(slot, buf, into, k):
        return pltpu.make_async_remote_copy(
            src_ref=buf.at[z],
            dst_ref=into.at[k],
            send_sem=ssem.at[slot, z],
            recv_sem=rsem.at[slot, k],
            device_id=along_z(k),
            device_id_type=MESH,
        )

    def to_row(slot, buf, into, d):
        to = lax.rem(z + d, nz)
        return pltpu.make_async_remote_copy(
            src_ref=buf.at[to],
            dst_ref=into.at[z],
            send_sem=ssem.at[slot, d],
            recv_sem=rsem.at[slot, z],
            device_id=along_z(to),
            device_id_type=MESH,
        )

    class Scan:
        def __init__(self, buf, into, back_buf, back_in):
            self.there, self.back = next(slots), next(slots)
            self.buf, self.into, self.back_buf, self.back_in = buf, into, back_buf, back_in

        def send(self, c):
            for t in heads_of(c):

                @pl.when(z != t)
                def _():
                    to_owner(self.there, self.buf, self.into, t).start()

                @pl.when(z == t)
                def _():
                    self.into[t] = self.buf[t]

        def scan(self, c, body):
            @pl.when((z >= bounds[c]) & (z < bounds[c + 1]))
            def _():
                for d in range(1, nz):
                    from_sender(self.there, self.buf, self.into, lax.rem(z + d, nz)).wait_recv()
                body()
                for d in sorted(range(1, nz), key=lambda d: -min(d, nz - d)):
                    to_row(self.back, self.back_buf, self.back_in, d).start()
                self.back_in[z] = self.back_buf[z]

        def wait(self, c):
            for t in heads_of(c):

                @pl.when(z != t)
                def _():
                    from_sender(self.back, self.back_buf, self.back_in, t).wait_recv()

        def sent(self):
            for t in range(nz):

                @pl.when(z != t)
                def _():
                    to_owner(self.there, self.buf, self.into, t).wait_send()

            for d in range(1, nz):
                to_row(self.back, self.back_buf, self.back_in, d).wait_send()

    forward = Scan(t_buf, t_in, zb_buf, zb_in)

    def compose(c):
        for j in heads_of(c):
            total = s_in[from_y(0), rows_z(j), :]
            for k in range(1, ny):
                total = f_ref[k, j : j + 1, :] * total + s_in[from_y(k), rows_z(j), :]
            t_buf[j] = total
        forward.send(c)

    def scan_forward():
        state = start_ref[...]
        for k in range(nz):
            zb_buf[k] = state
            state = fz_ref[k : k + 1, :] * state + t_in[k]
        fin_ref[...] = state

    def expand(c):
        forward.wait(c)
        for j in heads_of(c):
            state = zb_in[j]
            for k in range(ny):
                yb_buf[k, rows_z(j), :] = state
                if k < ny - 1:
                    state = f_ref[k, j : j + 1, :] * state + s_in[from_y(k), rows_z(j), :]
        send_y(yb_buf, yb_in, c, y_back)

    def read(j, _):
        cols = cols_of(j)
        inc = take_heads(yb_in, j).astype(BF)
        ssd = ssd_ref[:, cols] + e_ref[:, cols] * nt(r_ref[...], inc)
        ssd_ref[:, cols] = ssd
        v = ssd * (g_ref[:, cols].astype(F32) * sig_ref[:, cols])
        v_ref[:, cols] = v
        acc_ref[0] += v * v
        acc_ref[1] += v * (og_ref[:, cols].astype(F32) * gain_ref[:, cols])
        return 0

    y_there, y_back = [], []
    loaded(0, 2, 3)
    loop(first, 0)
    pl.semaphore_wait(barrier, partners)
    logs_y = exchange("y", at(lg_buf), at(lg_in))
    lg_in[0] = lg_buf[y]
    send_y(s_buf, s_in, 0, y_there)
    for c in range(1, CHUNKS):
        loop(first, c)
        send_y(s_buf, s_in, c, y_there)
    causal = iota((toks, toks), 0) >= iota((toks, toks), 1)
    rwm_ref[...] = jnp.where(causal, nt(r_ref[...], w_ref[...]), 0.0)
    rwt_ref[...] = jnp.where(
        iota((toks, toks), 0) <= iota((toks, toks), 1), nt(w_ref[...], r_ref[...]), 0.0
    )
    acc_ref[...] = jnp.zeros_like(acc_ref)
    arrived(logs_y)
    log_sum = jnp.zeros((8, N), F32)
    for k in range(ny):
        log_end = lg_in[from_y(k)]
        f_ref[k] = jnp.exp(log_end)
        log_sum = log_sum + log_end
    lr_buf[...] = log_sum
    logs_z = exchange("z", whole(lr_buf), at(lr_in))
    lr_in[0] = log_sum
    loaded(1, 8, 9, 10)
    arrived(y_there[0])
    compose(0)
    loop(intra, 0)
    arrived(y_there[1])
    compose(1)
    loop(intra, 1)
    arrived(y_there[2])
    compose(2)
    arrived(logs_z)
    for k in range(nz):
        fz_ref[k : k + 1, :] = jnp.exp(lr_in[from_z(k), pl.ds(z, 1), :])
    forward.scan(0, scan_forward)
    loop(intra, 2)
    arrived(y_there[3])
    compose(3)
    forward.scan(1, scan_forward)
    loop(intra, 3)
    forward.scan(2, scan_forward)
    expand(0)
    forward.scan(3, scan_forward)
    store(1)
    for c in range(1, 3):
        expand(c)
    arrived(y_back[0])
    loop(read, 0)
    expand(3)
    for c in range(1, CHUNKS):
        arrived(y_back[c])
        loop(read, c)
    tp_buf[0:1, :] = jnp.sum(jnp.transpose(acc_ref[0]), axis=0, keepdims=True)
    tp_buf[1:2, :] = jnp.sum(jnp.transpose(acc_ref[1]), axis=0, keepdims=True)
    tp_buf[2:, :] = jnp.zeros((6, toks), F32)
    tp_sums = exchange("t", whole(tp_buf), at(tp_in))
    tp_in[0] = tp_buf[...]
    arrived(tp_sums)
    both = tp_in[0]
    for k in range(1, ntp):
        both = both + tp_in[k]
    inverse = lax.rsqrt(both[0:1, :] / inner + EPS)
    slope = inverse * inverse * inverse * both[1:2, :] / inner
    invk_ref[0] = jnp.transpose(jnp.broadcast_to(inverse, (N, toks)))
    invk_ref[1] = jnp.transpose(jnp.broadcast_to(slope, (N, toks)))

    def back(j, _):
        cols = cols_of(j)
        sg = og_ref[:, cols].astype(F32) * gain_ref[:, cols]
        dv = invk_ref[0] * sg - v_ref[:, cols] * invk_ref[1]
        d = dv * (g_ref[:, cols].astype(F32) * sig_ref[:, cols])
        d_ref[:, cols] = d.astype(BF)
        de = (d * e_ref[:, cols]).astype(BF)
        de_ref[:, cols] = de
        put_heads(g_buf, j, tn(de, r_ref[...]))
        return 0

    rk_ref[...] = jnp.zeros_like(rk_ref)
    dwr_ref[...] = jnp.zeros_like(dwr_ref)
    drwt_ref[...] = jnp.zeros_like(drwt_ref)

    def gather_heads(j, prod):
        place = (
            iota((N, N), 1) == 2 * j + jnp.where(iota((N, N), 0) < P_SIZE, 0, 1)
        ).astype(F32).astype(BF)
        hi = prod.astype(BF)
        lo = (prod - hi.astype(F32)).astype(BF)
        return nn(hi, place) + nn(lo, place)

    def outs(j, _):
        cols = cols_of(j)
        og = og_ref[:, cols].astype(F32)
        gain = gain_ref[:, cols]
        v = v_ref[:, cols]
        ssd = ssd_ref[:, cols]
        vi = v * invk_ref[0]
        out_ref[:, cols] = (vi * gain).astype(BF)
        ny_buf[pl.ds(j, 1), :] = jnp.sum(og * vi, axis=0, keepdims=True)
        dv = invk_ref[0] * (og * gain) - v * invk_ref[1]
        gate = g_ref[:, cols].astype(F32)
        sig = sig_ref[:, cols]
        dg_ref[:, cols] = (dv * ssd * sig * (1.0 + gate * (1.0 - sig))).astype(BF)
        x = x_ref[:, cols].astype(F32)
        d = d_ref[:, cols].astype(F32)
        sk = jnp.sum(dv * (gate * sig) * x, axis=0, keepdims=True)
        sk_ref[pl.ds(2 * j, 1), :] = jnp.where(lane_low, sk, 0.0)
        sk_ref[pl.ds(2 * j + 1, 1), :] = jnp.where(lane_low, 0.0, sk)
        rk_ref[0] += gather_heads(j, d * (ssd - skip_of(j) * x))
        dwr_ref[1] += nn(de_ref[:, cols], take_heads(yb_in, j).astype(BF))
        return 0

    def intra_back(j, _):
        cols = cols_of(j)
        xd = xd_ref[:, cols]
        dp = d_ref[:, cols]
        made = []
        sums = None
        for i in range(2):
            h = 2 * j + i
            keep = lane_low if i == 0 else jnp.logical_not(lane_low)
            mine = jnp.where(keep, dp.astype(F32), 0.0).astype(BF)
            rhs = rhs_ref[h]
            decay = jnp.exp(jnp.minimum(-nn(lhs_ref[:half, :], rhs), 0.0))
            upper = nt(xd[:half], mine) * decay
            top = nn((rwt_ref[:half, :] * decay).astype(BF), dp)
            decay = jnp.exp(jnp.minimum(-nn(lhs_ref[half:, :], rhs[:, half:]), 0.0))
            lower = nt(xd[half:], mine[half:]) * decay
            low = nn((rwt_ref[half:, half:] * decay).astype(BF), dp[half:])
            made.append(jnp.concatenate([top, low], axis=0))
            sums = (upper, lower) if sums is None else (sums[0] + upper, sums[1] + lower)
        drwt_ref[:half, :] += sums[0]
        drwt_ref[half:, half:] += sums[1]
        unscaled = jnp.where(lane_low, made[0], made[1])
        v_ref[:, cols] = xd.astype(F32) * unscaled
        dxi_ref[:, cols] = unscaled * dl_ref[:, cols]
        return 0

    backward = Scan(u_buf, u_in, vb_buf, vb_in)

    def compose_back(c):
        for j in heads_of(c):
            total = g_in[from_y(ny - 1), rows_z(j), :]
            for k in range(ny - 2, -1, -1):
                total = f_ref[k, j : j + 1, :] * total + g_in[from_y(k), rows_z(j), :]
            u_buf[j] = total
        backward.send(c)

    def scan_back():
        state = jnp.zeros((P_SIZE, N), F32)
        for k in range(nz - 1, -1, -1):
            vb_buf[k] = state
            state = fz_ref[k : k + 1, :] * state + u_in[k]

    def expand_back(c):
        backward.wait(c)
        for j in heads_of(c):
            state = vb_in[j]
            for k in range(ny - 1, -1, -1):
                wb_buf[k, rows_z(j), :] = state
                if k > 0:
                    state = f_ref[k, j : j + 1, :] * state + g_in[from_y(k), rows_z(j), :]
        send_y(wb_buf, wb_in, c, w_back)

    g_there, w_back = [], []
    for c in range(CHUNKS):
        loop(back, c)
        send_y(g_buf, g_in, c, g_there)
    loop(outs, 0)
    arrived(g_there[0])
    compose_back(0)
    loop(outs, 1)
    arrived(g_there[1])
    compose_back(1)
    loop(outs, 2)
    arrived(g_there[2])
    compose_back(2)
    loop(outs, 3)
    store(0, 3)
    skip_sum = row_of(jnp.sum(sk_ref[...], axis=1, keepdims=True))
    ny_buf[pairs:, :] = jnp.zeros((ny_buf.shape[0] - pairs, N), F32)
    ny_buf[pairs : pairs + 1, :heads] = skip_sum
    sums_y = exchange("y", whole(ny_buf), at(ny_in))
    ny_in[0] = ny_buf[...]
    backward.scan(0, scan_back)
    loop(intra_back, 0)
    arrived(g_there[3])
    compose_back(3)
    backward.scan(1, scan_back)
    loop(intra_back, 1)
    backward.scan(2, scan_back)
    expand_back(0)
    loop(intra_back, 2)
    backward.scan(3, scan_back)
    for c in range(1, 3):
        expand_back(c)
    loop(intra_back, 3)
    expand_back(3)

    below = iota((toks, toks), 0) <= iota((toks, toks), 1)
    drwt = jnp.where(below, drwt_ref[...], 0.0).astype(BF)
    dr_in = tn(drwt, w_ref[...])
    dr_ref[...] = (dr_in.astype(BF).astype(F32) + dwr_ref[1].astype(BF).astype(F32)).astype(BF)
    store(5)
    dw_in = nn(drwt, r_ref[...])
    arrived(sums_y)
    total = ny_in[0]
    for k in range(1, ny):
        total = total + ny_in[k]
    nz_buf[...] = total
    sums_z = exchange("z", whole(nz_buf), at(nz_in))
    nz_in[0] = nz_buf[...]

    def last(j, _):
        cols = cols_of(j)
        later = take_heads(wb_in, j)
        inc = take_heads(yb_in, j)
        held = later * inc
        later = later.astype(BF)
        state_part = nt(w_ref[...], later) * te_ref[:, cols]
        x = x_ref[:, cols].astype(F32)
        written = x * state_part
        rk_ref[1] += gather_heads(j, v_ref[:, cols] + written)
        written = jnp.sum(written, axis=0, keepdims=True)
        for i in range(2):
            h = 2 * j + i
            factor = f_own[lax.rem(h, ny), pl.ds(lax.div(h, ny), 1), :]
            kept = jnp.sum(held[i * P_SIZE : (i + 1) * P_SIZE], axis=0, keepdims=True)
            keep = lane_low if i == 0 else jnp.logical_not(lane_low)
            es_ref[pl.ds(h, 1), :] = factor * kept + jnp.where(keep, written, 0.0)
        te_ref[:, cols] = state_part
        return 0

    def inputs_back(j, _):
        cols = cols_of(j)
        state_part = te_ref[:, cols]
        intra_part = dxi_ref[:, cols]
        direct = (d_ref[:, cols].astype(F32) * skip_of(j)).astype(BF).astype(F32)
        joined = (intra_part.astype(BF).astype(F32) + state_part.astype(BF).astype(F32)).astype(BF)
        dx_ref[:, cols] = (joined.astype(F32) + direct).astype(BF)
        dwr_ref[0] += nn(xs_ref[:, cols], take_heads(wb_in, j).astype(BF))
        return 0

    for c in range(CHUNKS):
        arrived(w_back[c])
        loop(last, c)
        if c < CHUNKS - 2:
            loop(inputs_back, c)

    k_rows = jnp.transpose(rk_ref[1])[:heads]
    d_log = jnp.transpose(rk_ref[0])[:heads] - k_rows
    end_sum = jnp.sum(es_ref[...], axis=1, keepdims=True)
    d_log = d_log + jnp.where(iota((heads, toks), 1) == toks - 1, end_sum, 0.0)
    from_on = (iota((toks, toks), 0) >= iota((toks, toks), 1)).astype(F32).astype(BF)
    d_inc = nn3(d_log, from_on)
    d_delta = k_rows / dl_row[...] - rate * d_inc
    again = raw_ref[...] + column(bias_ref[...])
    d_raw = d_delta * (1.0 / (1.0 + jnp.exp(-again)))
    dstep_ref[...] = d_raw
    ly_buf[...] = jnp.zeros_like(ly_buf)
    ly_buf[0:1, :heads] = row_of(jnp.sum(d_raw, axis=1, keepdims=True))
    ly_buf[1:2, :heads] = row_of(jnp.sum(d_inc * (-rate * dl_row[...]), axis=1, keepdims=True))
    late_y = exchange("y", whole(ly_buf), at(ly_in))
    ly_in[0] = ly_buf[...]
    for c in range(CHUNKS - 2, CHUNKS):
        loop(inputs_back, c)
    store(2, 6)
    dw_ref[...] = (dw_in.astype(BF).astype(F32) + dwr_ref[0].astype(BF).astype(F32)).astype(BF)
    store(4)
    arrived(late_y)
    total = ly_in[0]
    for k in range(1, ny):
        total = total + ly_in[k]
    lz_buf[...] = total
    late_z = exchange("z", whole(lz_buf), at(lz_in))
    lz_in[0] = lz_buf[...]
    arrived(sums_z)
    arrived(late_z)
    scale = 1.0 / math.sqrt(toks * ny * nz)
    total = nz_in[0]
    late = lz_in[0]
    for k in range(1, nz):
        total = total + nz_in[k]
        late = late + lz_in[k]
    for j in range(pairs):
        dnorm_ref[0:1, j * N : (j + 1) * N] = total[j : j + 1, :] * scale
    dheads_ref[0:2, :] = late[0:2, :heads] * scale
    dheads_ref[2:3, :] = total[pairs : pairs + 1, :heads] * scale
    store(7, 8)
    forward.sent()
    backward.sent()
    for made in started:
        sent(made)
    for made in stores:
        made.wait()


def copy_kernel(n, *refs):
    sources, places, held, sem = refs[:n], refs[n : 2 * n], refs[2 * n : 3 * n], refs[-1]
    made = []
    for i in range(n):
        load = pltpu.make_async_copy(sources[i], held[i], sem.at[0, i])
        load.start()
        made.append((load, pltpu.make_async_copy(held[i], places[i], sem.at[1, i])))
    for load, store in made:
        load.wait()
        store.start()
    for _, store in made:
        store.wait()


def solution(mesh):
    nctx, ntp = mesh.shape["ctx"], mesh.shape["tp"]
    ny, nz = NY, nctx // NY

    def on_device(
        inputs,
        gate_input,
        write_proj,
        read_proj,
        step_raw,
        step_bias,
        decay_log,
        skip_gain,
        norm_gain,
        start_state,
        out_grad,
    ):
        toks, cols = inputs.shape
        heads = step_raw.shape[0]
        pairs = heads // 2
        group = nz * P_SIZE
        f32, bf = F32, BF

        def v(shape, dtype=f32):
            return pltpu.VMEM(shape, dtype)

        scratch = [
            pltpu.SemaphoreType.DMA((2, 11)),
            v((toks, N), bf),
            v((toks, N), bf),
            v((toks, N), bf),
            v((heads, N, toks), bf),
            v((3, heads, toks)),
            v((heads, toks)),
            v((toks, cols)),
            v((toks, cols)),
            v((toks, cols)),
            v((toks, cols), bf),
            v((toks, cols), bf),
            v((toks, cols)),
            v((toks, cols)),
            v((toks, cols)),
            v((toks, cols), bf),
            v((toks, cols), bf),
            v((toks, cols)),
            v((toks, toks)),
            v((toks, toks)),
            v((toks, toks)),
            v((2, toks, N)),
            v((2, toks, N)),
            v((2, toks, N)),
            v((2, toks, N)),
            v((heads, N)),
            v((heads, N)),
            v((ny, 8, N)),
            v((ny, 8, N)),
            v((8, N)),
            v((nz, 8, N)),
            v((ny, 8, N)),
            v((ny, 8, N)),
            v((8, N)),
            v((ny, group, N)),
            v((ny, group, N)),
            v((nz, P_SIZE, N)),
            v((nz, P_SIZE, N)),
            v((nz, P_SIZE, N)),
            v((nz, P_SIZE, N)),
            v((ny, group, N)),
            v((ny, group, N)),
            v((ny, group, N)),
            v((ny, group, N)),
            v((nz, P_SIZE, N)),
            v((nz, P_SIZE, N)),
            v((nz, P_SIZE, N)),
            v((nz, P_SIZE, N)),
            v((ny, group, N)),
            v((ny, group, N)),
            v((8, toks)),
            v((ntp, 8, toks)),
            v((pairs + 8, N)),
            v((ny, pairs + 8, N)),
            v((pairs + 8, N)),
            v((nz, pairs + 8, N)),
            v((8, N)),
            v((ny, 8, N)),
            v((8, N)),
            v((nz, 8, N)),
            pltpu.SemaphoreType.DMA((SLOTS, 8)),
            pltpu.SemaphoreType.DMA((SLOTS, 8)),
        ]
        anywhere = pl.BlockSpec(memory_space=pl.ANY)
        shapes = [
            jax.ShapeDtypeStruct((toks, cols), bf),
            jax.ShapeDtypeStruct((P_SIZE, N), f32),
            jax.ShapeDtypeStruct((toks, cols), bf),
            jax.ShapeDtypeStruct((toks, cols), bf),
            jax.ShapeDtypeStruct((toks, N), bf),
            jax.ShapeDtypeStruct((toks, N), bf),
            jax.ShapeDtypeStruct((heads, toks), f32),
            jax.ShapeDtypeStruct((3, heads), f32),
            jax.ShapeDtypeStruct((1, cols), f32),
        ]
        operands = (
            inputs,
            gate_input,
            write_proj,
            read_proj,
            step_raw,
            step_bias.reshape(1, heads),
            decay_log.reshape(1, heads),
            skip_gain.reshape(1, heads),
            norm_gain.reshape(1, cols),
            start_state.reshape(P_SIZE, N),
            out_grad,
        )
        held_in = [v(a.shape, a.dtype) for a in operands]
        held_out = [v(a.shape, a.dtype) for a in shapes]

        def whole_kernel(*refs):
            kernel(ny, nz, ntp, refs[:11], refs[11:20], refs[20:31], refs[31:40], *refs[40:])

        made = pl.pallas_call(
            whole_kernel,
            out_shape=shapes,
            in_specs=[anywhere] * 11,
            out_specs=[anywhere] * 9,
            scratch_shapes=held_in + held_out + scratch,
            compiler_params=pltpu.CompilerParams(
                collective_id=0, has_side_effects=True, vmem_limit_bytes=60 * 2**20
            ),
        )(*operands)
        made = pl.pallas_call(
            functools.partial(copy_kernel, 9),
            out_shape=shapes,
            in_specs=[anywhere] * 9,
            out_specs=[anywhere] * 9,
            scratch_shapes=[v(a.shape, a.dtype) for a in shapes]
            + [pltpu.SemaphoreType.DMA((2, 9))],
        )(*made)
        output, final, dx, dg, dw, dr, dstep, dheads, dnorm = made
        return (
            output,
            final.reshape(1, 1, P_SIZE * N),
            dx,
            dg,
            dw,
            dr,
            dstep,
            dheads,
            dnorm.reshape(cols),
        )

    in_specs = (
        P("ctx", "tp"),
        P("ctx", "tp"),
        P("ctx", "tp"),
        P("ctx", "tp"),
        P("tp", "ctx"),
        P("tp"),
        P("tp"),
        P("tp"),
        P("tp"),
        P("tp", "ctx", None),
        P("ctx", "tp"),
    )
    out_specs = (
        P("ctx", "tp"),
        P("tp", "ctx", None),
        P("ctx", "tp"),
        P("ctx", "tp"),
        P("ctx", "tp"),
        P("ctx", "tp"),
        P("tp", "ctx"),
        P(None, "tp"),
        P("tp"),
    )
    return jax.shard_map(
        on_device, mesh=mesh, in_specs=in_specs, out_specs=out_specs, check_vma=False
    )
```
